32 devices in a mesh: parts: 2 (over y), cls: 16 (over z, x, core).
Axes of the slice: x: 2, y: 2, z: 4, core: 2. Of those that a mesh axis runs over, the one named last changes fastest.
Arguments:
- images: bfloat16 [2048, 128, 128], P(('parts', 'cls')), parts along dimension 0, may hold values from -6 to 6
- mask_radius: int32 [2048], P(('parts', 'cls')), parts along dimension 0, may hold values from 40 to 64
- rotation_prior: int32 [2048], P(('parts', 'cls')), parts along dimension 0, may hold values from 0 to 63
- candidates: int32 [2048, 8], P(('parts', 'cls')), parts along dimension 0, may hold values from 0 to 31, all different within a row; in each aligned block of 64 rows (0 to 63, 64 to 127, ...) at most 32 rows name the same one
- references: bfloat16 [64, 64, 4096], P(('parts', 'cls')), parts along dimension 0, may hold values from -0.19921875 to 0.19921875
- noise_inverse_power: float32 [2048], replicated, may hold values from 0.5 to 2
- class_bias: float32 [64], P(('parts', 'cls')), parts along dimension 0, may hold values from -1.5 to 300
Outputs:
- class_sums: float32 [64, 64, 4096], P(('parts', 'cls')), parts along dimension 0
- occupancy: float32 [64, 64], P(('parts', 'cls')), parts along dimension 0
- log_norm: float32 [2048], P(('parts', 'cls')), parts along dimension 0
The draws below stay inside these ranges and needn't reach their ends.
There are 2 independent parts, one for each index of `parts`. The reference program is written for one: setup_inputs(seed, part) draws one part's arguments, and reference() takes and returns one part's arrays. A program takes and returns all parts, laid end to end along the dimension named above; an argument that names none is the same for every part. Nothing has to cross between parts.
Inputs may be any that keep to these rules, and one draw needn't show every extreme that they name: `candidates`: each row names 8 different classes. Among the rows of one device no class is named more than 32 times, a bound that some block reaches.
All inputs are finite; a program needn't handle non-finite values.
Results may differ from the reference program's by a relative error of at most 0.0097.
Values may be sent and summed in bfloat16 or wider, within the bound.
A program may use at most 128 MiB of HBM per device.

```python
import math
import jax
import jax.numpy as jnp
import numpy as np
from jax import lax

PIX = 128
BAND = 32
ROT = 64
SIDE = 3
K = 8
C_DEV = 2
P_DEV = 64
CLASSES = 32
PARTICLES = 1024
FREQ = 4096
M = 32
N_CLS = 16


def draw_class_bias(key, part):
    key = jax.random.fold_in(key, 11)
    base_values = jax.random.uniform(jax.random.fold_in(key, 1), (CLASSES,), jnp.float32, -1.5, 1.5)
    return base_values


def set_ends(entries, key, low, largest):
    longest = entries.shape.index(max(entries.shape))
    spots = []
    for shift in (0, 1):
        where = [jax.random.randint(jax.random.fold_in(key, axis), (), 0, length) for axis, length in enumerate(entries.shape)]
        where[longest] = (where[longest] + shift) % entries.shape[longest]
        spots.append(tuple(where))
    return entries.at[spots[0]].set(low).at[spots[1]].set(largest)


def block_levels(stream_key, extent, pieces, smallest, high):
    factor_of = 1.0
    for axis_at, blocks in pieces:
        steps = jax.random.uniform(jax.random.fold_in(jax.random.fold_in(stream_key, 6), axis_at), (blocks,), jnp.float32, smallest / len(pieces), high / len(pieces))
        factor_of = factor_of * jnp.repeat(jnp.exp(steps), extent[axis_at] // blocks).reshape((-1,) + (1,) * (len(extent) - 1 - axis_at))
    return factor_of


def routed_block(stream_key, own, number, rows, amount, top, bound, skew):
    sequence = jax.random.permutation(stream_key, amount)
    heavy_load, ordinary = load_shares(amount, rows * top, bound, skew, True), load_shares(amount, rows * top, bound, skew, False)
    places = jnp.arange(amount)

    def named(lengths, rotation):
        used = int((lengths > 0).sum())
        fixed = max(1, used // 4)
        shifted = fixed + (places - fixed + rotation * (used - fixed)) % max(1, amount - fixed)
        return jnp.zeros((amount,), jnp.int32).at[sequence[jnp.where(places < fixed, places, shifted)]].set(jnp.asarray(lengths, jnp.int32))

    lengths = jnp.where(number % 4 == 0, named(heavy_load, number // 4), named(ordinary, number - number // 4 - 1))
    mixed = jax.random.permutation(jax.random.fold_in(own, 3), amount)
    giver, sink = mixed[0:amount // 2 * 2:2], mixed[1:amount // 2 * 2:2]
    room = jnp.minimum(lengths[giver] - 1, bound - lengths[sink]) // 2
    room = jnp.where((giver == sequence[0]) | (sink == sequence[0]) | (lengths[sink] == 0), 0, jnp.maximum(room, 0))
    shifted = jax.random.randint(jax.random.fold_in(own, 4), (amount // 2,), 0, 1 << 20) % (room + 1)
    lengths = lengths.at[giver].add(-shifted).at[sink].add(shifted)
    members = jnp.searchsorted(jnp.cumsum(lengths), jnp.arange(rows * top), side="right").astype(jnp.int32)
    grid = members.reshape(top, rows).T
    grid = grid[jax.random.permutation(jax.random.fold_in(own, 1), rows)]
    rotation = jax.random.randint(jax.random.fold_in(own, 2), (rows, 1), 0, top)
    return jnp.take_along_axis(grid, (jnp.arange(top)[None, :] + rotation) % top, axis=1)


def load_shares(number_of, total, most, lean, full):
    portions = [(1 << 20) // math.isqrt(standing ** lean) + 1 for standing in range(1, number_of + 1)]
    largest = most if full else min(most, max(-(-total // number_of), total * portions[0] // sum(portions)))
    least = 1 if total - largest >= number_of - 1 else 0
    given, rest = [largest] + [least] * (number_of - 1), total - largest - least * (number_of - 1)
    while rest > 0:
        free = [i for i in range(1, number_of) if given[i] < largest] or [i for i in range(1, number_of) if given[i] < most]
        pool, left = sum([portions[i] for i in free]), rest
        for i in free:
            more = min(most - given[i], max(1, left * portions[i] // pool), rest)
            given[i] = given[i] + more
            rest = rest - more
    return np.array(given)


def noise(key, extent, spread, reach, shards=(), kind=jnp.bfloat16):
    factor_of = block_levels(key, extent, shards, -0.22, 0.18) if shards else 1.0
    result = jax.random.normal(key, extent, jnp.float32) * spread * factor_of
    return jnp.minimum(jnp.maximum(result, -reach), reach).astype(kind)


def setup_inputs(seed: int = 0, part: int = 0) -> dict:
    streams_of = jax.random.split(jax.random.key(seed), 8)
    part_splits = jax.random.split(jax.random.fold_in(streams_of[7], part), 8)
    images = noise(part_splits[0], (PARTICLES, PIX, PIX), 1.0, 6.0, ((0, 16),))
    mask_radius = set_ends(jax.random.randint(part_splits[1], (PARTICLES,), PIX * 5 // 16, PIX // 2 + 1), jax.random.fold_in(part_splits[1], 1), PIX * 5 // 16, (PIX // 2 + 1) - 1).astype(jnp.int32)
    rotation_prior = set_ends(jax.random.randint(part_splits[2], (PARTICLES,), 0, ROT), jax.random.fold_in(part_splits[2], 1), 0, ROT - 1).astype(jnp.int32)
    candidates_keys = jax.random.split(jax.random.fold_in(part_splits[3], 1), PARTICLES // P_DEV)
    candidates_turns = jax.random.permutation(jax.random.fold_in(part_splits[3], 3), PARTICLES // P_DEV)
    candidates = jax.vmap(lambda own, number: routed_block(jax.random.fold_in(part_splits[3], 2), own, number, P_DEV, CLASSES, K, M, 2))(candidates_keys, candidates_turns).reshape((PARTICLES, K))
    references = noise(part_splits[4], (CLASSES, ROT, FREQ), 0.03, 0.19921875, ((0, 16),))
    noise_inverse_power = jnp.clip(jnp.exp(jax.random.uniform(streams_of[5], (2 * BAND * BAND,), jnp.float32, math.log(0.5), math.log(2.0))), 0.5, 2.0)
    class_bias = draw_class_bias(jax.random.fold_in(jax.random.fold_in(streams_of[7], part), 71), part)
    return {"images": images, "mask_radius": mask_radius, "rotation_prior": rotation_prior, "candidates": candidates, "references": references, "noise_inverse_power": noise_inverse_power, "class_bias": class_bias}


KAPPA = 2.0


def dft_tables(pixels, band_size):
    pixel_idx = jnp.arange(pixels, dtype=jnp.int32)
    freq_x = jnp.arange(band_size, dtype=jnp.int32)
    angles_x = (2.0 * math.pi / pixels) * ((pixel_idx[:, None] * freq_x[None, :]) % pixels).astype(jnp.float32)
    row_table = jnp.concatenate([jnp.cos(angles_x), -jnp.sin(angles_x)], axis=1).astype(jnp.bfloat16)
    freq_y = jnp.arange(2 * band_size, dtype=jnp.int32) - band_size
    angles_y = (2.0 * math.pi / pixels) * ((freq_y[:, None] * pixel_idx[None, :]) % pixels).astype(jnp.float32)
    cos_y = jnp.cos(angles_y)
    sin_y = jnp.sin(angles_y)
    upper = jnp.concatenate([cos_y, sin_y], axis=1)
    lower = jnp.concatenate([-sin_y, cos_y], axis=1)
    col_table = jnp.concatenate([upper, lower], axis=0).astype(jnp.bfloat16)
    return row_table, col_table


def spectra_of(images, mask_radius, row_table, col_table):
    row_count, pixels, _ = images.shape
    band_size = row_table.shape[1] // 2
    centre = jnp.arange(pixels, dtype=jnp.int32) - pixels // 2
    radius_sq = centre[:, None] * centre[:, None] + centre[None, :] * centre[None, :]
    inside = radius_sq[None, :, :] <= (mask_radius * mask_radius)[:, None, None]
    masked = jnp.where(inside, images, jnp.zeros((), jnp.bfloat16))
    partial_value = jnp.dot(masked.reshape(row_count * pixels, pixels), row_table, preferred_element_type=jnp.float32)
    partial_value = partial_value.astype(jnp.bfloat16).reshape(row_count, pixels, 2, band_size)
    partial_value = partial_value.transpose(0, 2, 1, 3).reshape(row_count, 2 * pixels, band_size)
    whole = jnp.einsum('ym,pmx->pyx', col_table.astype(jnp.float32), partial_value.astype(jnp.float32)) / pixels
    return whole.reshape(row_count, 4 * band_size * band_size).astype(jnp.bfloat16)


def phase_tables(pixels, band_size, side_len):
    freq_y = jnp.arange(2 * band_size, dtype=jnp.int32) - band_size
    freq_x = jnp.arange(band_size, dtype=jnp.int32)
    offsets = jnp.arange(side_len, dtype=jnp.int32) - side_len // 2
    shift_y = jnp.repeat(offsets, side_len)
    horizontal_displacement = jnp.tile(offsets, side_len)
    phase_arg = (freq_y[None, :, None] * shift_y[:, None, None] + freq_x[None, None, :] * horizontal_displacement[:, None, None]) % pixels
    angles = (2.0 * math.pi / pixels) * phase_arg.astype(jnp.float32).reshape(side_len * side_len, -1)
    return jnp.cos(angles), jnp.sin(angles)


def translated_images(reference_block, noise_inverse_power, cosine_lookup_matrix, sine_lookup_matrix):
    half_len = reference_block.shape[-1] // 2
    real_part = reference_block[:, :half_len].astype(jnp.float32) * noise_inverse_power[None, :]
    imag_part = reference_block[:, half_len:].astype(jnp.float32) * noise_inverse_power[None, :]
    cos_b = cosine_lookup_matrix[:, None, :]
    sin_b = sine_lookup_matrix[:, None, :]
    rot_real = real_part[None] * cos_b - imag_part[None] * sin_b
    turned_sine_term = real_part[None] * sin_b + imag_part[None] * cos_b
    stack = jnp.concatenate([rot_real, turned_sine_term], axis=-1).astype(jnp.bfloat16)
    return stack.reshape(-1, reference_block.shape[-1])


def penalty_lookup(reference_block, noise_inverse_power):
    half_len = reference_block.shape[-1] // 2
    real_part = reference_block[:, :half_len].astype(jnp.float32)
    imag_part = reference_block[:, half_len:].astype(jnp.float32)
    return 0.5 * jnp.sum(noise_inverse_power[None, :] * (real_part * real_part + imag_part * imag_part), axis=1)


def score_slots(block_spectra, centres, stack, penalty, bias_value, rot_count):
    slot_count = block_spectra.shape[0]
    cross_term = jnp.dot(block_spectra, stack.T, preferred_element_type=jnp.float32)
    cross_term = cross_term.reshape(slot_count, -1, rot_count)
    angle_step = jnp.arange(rot_count, dtype=jnp.float32)[None, :] - centres[:, None]
    prior_term = KAPPA * jnp.cos((2.0 * math.pi / rot_count) * angle_step)
    total = cross_term - penalty[None, None, :] + bias_value + prior_term[:, None, :]
    return total.reshape(slot_count, -1)


def shift_back(gathered, cosine_lookup_matrix, sine_lookup_matrix):
    half_len = gathered.shape[-1] // 2
    fragment_cosine_term = gathered[..., :half_len]
    part_imag = gathered[..., half_len:]
    cos_b = cosine_lookup_matrix[:, None, :]
    sin_b = sine_lookup_matrix[:, None, :]
    cosine_accumulation = jnp.sum(fragment_cosine_term * cos_b + part_imag * sin_b, axis=0)
    imaginary_running_sum = jnp.sum(part_imag * cos_b - fragment_cosine_term * sin_b, axis=0)
    return jnp.concatenate([cosine_accumulation, imaginary_running_sum], axis=-1)


def reference(images, mask_radius, rotation_prior, candidates, references, noise_inverse_power, class_bias):
    row_table, col_table = dft_tables(PIX, BAND)
    spectra = spectra_of(images, mask_radius, row_table, col_table)
    cosine_lookup_matrix, sine_lookup_matrix = phase_tables(PIX, BAND, SIDE)
    block_len = P_DEV * K
    flat_ids = candidates.reshape(N_CLS, block_len)
    placement_coordinate = jnp.arange(block_len, dtype=jnp.int32)
    same = (flat_ids[:, None, :] == flat_ids[:, :, None]) & (placement_coordinate[None, None, :] < placement_coordinate[None, :, None])
    earlier = jnp.sum(same.astype(jnp.int32), axis=2).astype(jnp.int32)
    source = jnp.arange(N_CLS, dtype=jnp.int32)[:, None]
    bucket = ((flat_ids * N_CLS + source) * M + earlier).reshape(-1).astype(jnp.int32)
    entry = jnp.arange(PARTICLES * K, dtype=jnp.int32)
    slot_total = N_CLS * M
    filled = jnp.zeros((CLASSES * slot_total,), jnp.int32).at[bucket].set(entry + 1)
    filled = filled.reshape(CLASSES, slot_total)

    def class_scores(inputs):
        reference_block, bias_value, slots = inputs
        live_slot = slots > 0
        row_id = jnp.maximum(slots - 1, 0) // K
        block_spectra = jnp.where(live_slot[:, None], spectra[row_id], jnp.zeros((), jnp.bfloat16))
        centres = rotation_prior[row_id].astype(jnp.float32)
        stack = translated_images(reference_block, noise_inverse_power, cosine_lookup_matrix, sine_lookup_matrix)
        penalty = penalty_lookup(reference_block, noise_inverse_power)
        return score_slots(block_spectra, centres, stack, penalty, bias_value, ROT)

    scores = lax.map(class_scores, (references, class_bias, filled))
    self_class_scores = scores.reshape(CLASSES * slot_total, -1)[bucket]
    per_particle = self_class_scores.reshape(PARTICLES, -1)
    peak_score = jnp.max(per_particle, axis=1)
    log_norm = peak_score + jnp.log(jnp.sum(jnp.exp(per_particle - peak_score[:, None]), axis=1))
    weights = jnp.exp(self_class_scores - jnp.repeat(log_norm, K)[:, None]).astype(jnp.bfloat16)
    output_scale_factor = C_DEV * ROT / P_DEV

    def class_sums_of(inputs):
        slots = inputs
        live_slot = slots > 0
        row_index = jnp.maximum(slots - 1, 0)
        block_weights = jnp.where(live_slot[:, None], weights[row_index], jnp.zeros((), jnp.bfloat16))
        block_spectra = jnp.where(live_slot[:, None], spectra[row_index // K], jnp.zeros((), jnp.bfloat16))
        occupied = jnp.sum(block_weights.astype(jnp.float32).reshape(slot_total, SIDE * SIDE, ROT), axis=(0, 1))
        gathered = jnp.dot(block_weights.T, block_spectra, preferred_element_type=jnp.float32)
        gathered = gathered.reshape(SIDE * SIDE, ROT, FREQ)
        return shift_back(gathered, cosine_lookup_matrix, sine_lookup_matrix) * output_scale_factor, occupied * output_scale_factor

    class_sums, occupancy = lax.map(class_sums_of, filled)
    return class_sums, occupancy, log_norm
```

```python
import functools
import math

import jax
import jax.numpy as jnp
from jax import lax
from jax.sharding import PartitionSpec as P

BAND = 32
SIDE = 3


KAPPA = 2.0
LOWEST = -1e30


def dft_tables(pixels, band_size):
    pixel_idx = jnp.arange(pixels, dtype=jnp.int32)
    freq_x = jnp.arange(band_size, dtype=jnp.int32)
    angles_x = (
        2.0 * math.pi / pixels * (pixel_idx[:, None] * freq_x[None, :] % pixels).astype(jnp.float32)
    )
    row_table = jnp.concatenate([jnp.cos(angles_x), -jnp.sin(angles_x)], axis=1).astype(
        jnp.bfloat16
    )
    freq_y = jnp.arange(2 * band_size, dtype=jnp.int32) - band_size
    angles_y = (
        2.0 * math.pi / pixels * (freq_y[:, None] * pixel_idx[None, :] % pixels).astype(jnp.float32)
    )
    cos_y = jnp.cos(angles_y)
    sin_y = jnp.sin(angles_y)
    upper = jnp.concatenate([cos_y, sin_y], axis=1)
    lower = jnp.concatenate([-sin_y, cos_y], axis=1)
    col_table = jnp.concatenate([upper, lower], axis=0).astype(jnp.bfloat16)
    return (row_table, col_table)


def spectra_of(images, mask_radius, row_table, col_table):
    row_count, pixels, _ = images.shape
    band_size = row_table.shape[1] // 2
    centre = jnp.arange(pixels, dtype=jnp.int32) - pixels // 2
    radius_sq = centre[:, None] * centre[:, None] + centre[None, :] * centre[None, :]
    inside = radius_sq[None, :, :] <= (mask_radius * mask_radius)[:, None, None]
    masked = jnp.where(inside, images, jnp.zeros((), jnp.bfloat16))
    partial_value = jnp.dot(
        masked.reshape(row_count * pixels, pixels), row_table, preferred_element_type=jnp.float32
    )
    partial_value = partial_value.astype(jnp.bfloat16).reshape(row_count, pixels, 2, band_size)
    partial_value = partial_value.transpose(0, 2, 1, 3).reshape(row_count, 2 * pixels, band_size)
    whole = (
        jnp.einsum("ym,pmx->pyx", col_table, partial_value, preferred_element_type=jnp.float32)
        / pixels
    )
    return whole.reshape(row_count, 4 * band_size * band_size).astype(jnp.bfloat16)


def phase_tables(pixels, band_size, side_len):
    freq_y = jnp.arange(2 * band_size, dtype=jnp.int32) - band_size
    freq_x = jnp.arange(band_size, dtype=jnp.int32)
    offsets = jnp.arange(side_len, dtype=jnp.int32) - side_len // 2
    shift_y = jnp.repeat(offsets, side_len)
    horizontal_displacement = jnp.tile(offsets, side_len)
    phase_arg = (
        freq_y[None, :, None] * shift_y[:, None, None]
        + freq_x[None, None, :] * horizontal_displacement[:, None, None]
    ) % pixels
    angles = 2.0 * math.pi / pixels * phase_arg.astype(jnp.float32).reshape(side_len * side_len, -1)
    return (jnp.cos(angles), jnp.sin(angles))


def translated_images(
    reference_block, noise_inverse_power, cosine_lookup_matrix, sine_lookup_matrix
):
    half_len = reference_block.shape[-1] // 2
    real_part = reference_block[:, :half_len].astype(jnp.float32) * noise_inverse_power[None, :]
    imag_part = reference_block[:, half_len:].astype(jnp.float32) * noise_inverse_power[None, :]
    cos_b = cosine_lookup_matrix[:, None, :]
    sin_b = sine_lookup_matrix[:, None, :]
    rot_real = real_part[None] * cos_b - imag_part[None] * sin_b
    turned_sine_term = real_part[None] * sin_b + imag_part[None] * cos_b
    stack = jnp.concatenate([rot_real, turned_sine_term], axis=-1).astype(jnp.bfloat16)
    return stack.reshape(-1, reference_block.shape[-1])


def penalty_lookup(reference_block, noise_inverse_power):
    half_len = reference_block.shape[-1] // 2
    real_part = reference_block[:, :half_len].astype(jnp.float32)
    imag_part = reference_block[:, half_len:].astype(jnp.float32)
    return 0.5 * jnp.sum(
        noise_inverse_power[None, :] * (real_part * real_part + imag_part * imag_part), axis=1
    )


def score_slots(block_spectra, centres, stack, penalty, bias_value, rot_count):
    slot_count = block_spectra.shape[0]
    cross_term = jnp.dot(block_spectra, stack.T, preferred_element_type=jnp.float32)
    cross_term = cross_term.reshape(slot_count, -1, rot_count)
    angle_step = jnp.arange(rot_count, dtype=jnp.float32)[None, :] - centres[:, None]
    prior_term = KAPPA * jnp.cos(2.0 * math.pi / rot_count * angle_step)
    total = cross_term - penalty[None, None, :] + bias_value + prior_term[:, None, :]
    return total.reshape(slot_count, -1)


def shift_back(gathered, cosine_lookup_matrix, sine_lookup_matrix):
    half_len = gathered.shape[-1] // 2
    real_block_part = gathered[..., :half_len]
    imaginary_block_part = gathered[..., half_len:]
    largest_score_seen = lax.Precision.HIGHEST
    real_running_sum = jnp.einsum(
        "iqz,iz->qz", real_block_part, cosine_lookup_matrix, precision=largest_score_seen
    ) + jnp.einsum(
        "iqz,iz->qz", imaginary_block_part, sine_lookup_matrix, precision=largest_score_seen
    )
    imaginary_running_sum = jnp.einsum(
        "iqz,iz->qz", imaginary_block_part, cosine_lookup_matrix, precision=largest_score_seen
    ) - jnp.einsum("iqz,iz->qz", real_block_part, sine_lookup_matrix, precision=largest_score_seen)
    return jnp.concatenate([real_running_sum, imaginary_running_sum], axis=-1)


def routed(
    images, mask_radius, rotation_prior, candidates, references, noise_inverse_power, class_bias
):
    row_count = images.shape[0]
    classes_on_device, rot_count, freq_len = references.shape
    top_count = candidates.shape[1]
    devices = lax.axis_size("cls")
    reference_groups_list = classes_on_device * devices
    maximum_holding = max(2, 2 * row_count * top_count // reference_groups_list)
    hypotheses = SIDE * SIDE * rot_count
    row_table, col_table = dft_tables(images.shape[1], BAND)
    spectra = spectra_of(images, mask_radius, row_table, col_table)
    cosine_lookup_matrix, sine_lookup_matrix = phase_tables(images.shape[1], BAND, SIDE)
    flat_ids = candidates.reshape(-1)
    placement_coordinate = jnp.arange(row_count * top_count, dtype=jnp.int32)
    same = (flat_ids[None, :] == flat_ids[:, None]) & (
        placement_coordinate[None, :] < placement_coordinate[:, None]
    )
    earlier = jnp.sum(same.astype(jnp.int32), axis=1)
    slot_index = flat_ids * maximum_holding + earlier
    filled = (
        jnp.zeros((reference_groups_list * maximum_holding,), jnp.int32)
        .at[slot_index]
        .set(placement_coordinate + 1)
    )
    live_slot = filled > 0
    entry_index = jnp.maximum(filled - 1, 0)
    owner_row = entry_index // top_count
    outgoing = jnp.where(live_slot[:, None], spectra[owner_row], jnp.zeros((), jnp.bfloat16))
    outgoing = outgoing.reshape(devices, classes_on_device, maximum_holding, freq_len)
    centres_out = jnp.where(live_slot, rotation_prior[owner_row], 0).astype(jnp.bfloat16)
    centres_out = centres_out.reshape(devices, classes_on_device, maximum_holding)
    stacks = [
        translated_images(
            references[device_local], noise_inverse_power, cosine_lookup_matrix, sine_lookup_matrix
        )
        for device_local in range(classes_on_device)
    ]
    displacement_costs = [
        penalty_lookup(references[device_local], noise_inverse_power)
        for device_local in range(classes_on_device)
    ]
    arrived, arrived_centres = (
        lax.all_to_all(outgoing, "cls", split_axis=0, concat_axis=0, tiled=True),
        lax.all_to_all(centres_out, "cls", split_axis=0, concat_axis=0, tiled=True),
    )
    sources = arrived.shape[0]
    width = arrived.shape[2]
    blocks = []
    for score_device_local in range(classes_on_device):
        score_block_spectra = arrived[:, score_device_local].reshape(sources * width, freq_len)
        centres = (
            arrived_centres[:, score_device_local].reshape(sources * width).astype(jnp.float32)
        )
        scored = score_slots(
            score_block_spectra,
            centres,
            stacks[score_device_local],
            displacement_costs[score_device_local],
            class_bias[score_device_local],
            rot_count,
        )
        blocks.append(scored.reshape(sources, width, hypotheses))
    scores = jnp.stack(blocks, axis=1)
    returned = lax.all_to_all(scores, "cls", split_axis=0, concat_axis=0, tiled=True)
    self_class_scores = returned.reshape(reference_groups_list * maximum_holding, hypotheses)[
        slot_index
    ]
    per_particle = self_class_scores.reshape(row_count, top_count * hypotheses)
    top_peak = jnp.max(per_particle, axis=1)
    log_norm = top_peak + jnp.log(jnp.sum(jnp.exp(per_particle - top_peak[:, None]), axis=1))
    own_weights = jnp.exp(self_class_scores - jnp.repeat(log_norm, top_count)[:, None]).astype(
        jnp.bfloat16
    )
    weight_buffer = jnp.where(
        live_slot[:, None], own_weights[entry_index], jnp.zeros((), jnp.bfloat16)
    )
    weight_buffer = weight_buffer.reshape(devices, classes_on_device, maximum_holding, hypotheses)
    weights = lax.all_to_all(weight_buffer, "cls", split_axis=0, concat_axis=0, tiled=True)
    output_scale_factor = classes_on_device * rot_count / row_count
    sum_list = []
    occ_list = []
    for device_local in range(classes_on_device):
        block_weights = weights[:, device_local].reshape(-1, hypotheses)
        block_spectra = arrived[:, device_local].reshape(-1, freq_len)
        occupied = jnp.sum(
            block_weights.astype(jnp.float32).reshape(-1, SIDE * SIDE, rot_count), axis=(0, 1)
        )
        occ_list.append(occupied * output_scale_factor)
        gathered = jnp.einsum(
            "sh,sf->hf", block_weights, block_spectra, preferred_element_type=jnp.float32
        )
        gathered = gathered.reshape(SIDE * SIDE, rot_count, freq_len)
        sum_list.append(
            shift_back(gathered, cosine_lookup_matrix, sine_lookup_matrix) * output_scale_factor
        )
    return (jnp.stack(sum_list, axis=0), jnp.stack(occ_list, axis=0), log_norm)


def dense(
    images, mask_radius, rotation_prior, candidates, references, noise_inverse_power, class_bias
):
    row_count, top_count = candidates.shape
    classes_on_device, rot_count, freq_len = references.shape
    devices = lax.axis_size("cls")
    hypotheses = SIDE * SIDE * rot_count
    me = lax.axis_index("cls")
    labels = jnp.concatenate([candidates, rotation_prior[:, None]], axis=1)
    all_labels = lax.all_gather(labels, "cls", axis=0, tiled=True)
    row_table, col_table = dft_tables(images.shape[1], BAND)
    spectra = spectra_of(images, mask_radius, row_table, col_table)
    everyone = lax.all_gather(spectra, "cls", axis=0, tiled=True)
    cos_t, sin_t = phase_tables(images.shape[1], BAND, SIDE)
    angle_step = (
        jnp.arange(rot_count, dtype=jnp.float32)[None, :]
        - all_labels[:, top_count].astype(jnp.float32)[:, None]
    )
    prior_term = KAPPA * jnp.cos(2.0 * math.pi / rot_count * angle_step)
    prior_term = jnp.tile(prior_term, (1, SIDE * SIDE))
    scores, names = [], []
    for c in range(classes_on_device):
        stack = translated_images(references[c], noise_inverse_power, cos_t, sin_t)
        penalty = penalty_lookup(references[c], noise_inverse_power)
        cross = jnp.dot(everyone, stack.T, preferred_element_type=jnp.float32)
        offset = jnp.tile(class_bias[c] - penalty, SIDE * SIDE)
        scores.append(cross + offset[None, :] + prior_term)
        names.append(jnp.any(all_labels[:, :top_count] == me * classes_on_device + c, axis=1))
    tops = [jnp.where(n, jnp.max(s, axis=1), LOWEST) for s, n in zip(scores, names)]
    top = functools.reduce(jnp.maximum, tops)
    mass = sum(
        jnp.where(n, jnp.sum(jnp.exp(s - jnp.where(n, top, jnp.inf)[:, None]), axis=1), 0.0)
        for s, n in zip(scores, names)
    )
    pairs = lax.all_gather(jnp.stack([top, mass]), "cls", axis=0)
    peak = jnp.max(pairs[:, 0], axis=0)
    norm = peak + jnp.log(jnp.sum(pairs[:, 1] * jnp.exp(pairs[:, 0] - peak[None]), axis=0))
    scale = classes_on_device * rot_count / row_count
    sums, occ = [], []
    for s, n in zip(scores, names):
        limit = jnp.where(n, norm, jnp.inf)
        weights = jnp.exp(s - limit[:, None]).astype(jnp.bfloat16)
        occ.append(
            scale
            * jnp.sum(
                weights.astype(jnp.float32).reshape(-1, SIDE * SIDE, rot_count), axis=(0, 1)
            )
        )
        gathered = jnp.einsum("sh,sf->hf", weights, everyone, preferred_element_type=jnp.float32)
        gathered = gathered.reshape(SIDE * SIDE, rot_count, freq_len)
        sums.append(shift_back(gathered, cos_t, sin_t) * scale)
    own = lax.dynamic_slice(norm, (me * row_count,), (row_count,))
    return (jnp.stack(sums, axis=0), jnp.stack(occ, axis=0), own)


def local(*arrays):
    row_count, top_count = arrays[3].shape
    classes = arrays[4].shape[0] * lax.axis_size("cls")
    slots = max(2, 2 * row_count * top_count // classes)
    return dense(*arrays) if row_count <= 2 * slots else routed(*arrays)


def solution(mesh):
    in_specs = (
        P(("parts", "cls"), None, None),
        P(("parts", "cls")),
        P(("parts", "cls")),
        P(("parts", "cls"), None),
        P(("parts", "cls"), None, None),
        P(),
        P(("parts", "cls")),
    )
    out_specs = (P(("parts", "cls"), None, None), P(("parts", "cls"), None), P(("parts", "cls")))
    return jax.shard_map(local, mesh=mesh, in_specs=in_specs, out_specs=out_specs, check_vma=False)
```

```python
import functools
import math

import jax
import jax.numpy as jnp
import numpy as np
from jax import lax
from jax.experimental import pallas as pl
from jax.experimental.pallas import tpu as pltpu
from jax.sharding import PartitionSpec as P

BAND = 32
SIDE = 3


KAPPA = 2.0
LOWEST = -1e30


def dft_tables(pixels, band_size):
    pixel_idx = jnp.arange(pixels, dtype=jnp.int32)
    freq_x = jnp.arange(band_size, dtype=jnp.int32)
    angles_x = (
        2.0 * math.pi / pixels * (pixel_idx[:, None] * freq_x[None, :] % pixels).astype(jnp.float32)
    )
    row_table = jnp.concatenate([jnp.cos(angles_x), -jnp.sin(angles_x)], axis=1).astype(
        jnp.bfloat16
    )
    freq_y = jnp.arange(2 * band_size, dtype=jnp.int32) - band_size
    angles_y = (
        2.0 * math.pi / pixels * (freq_y[:, None] * pixel_idx[None, :] % pixels).astype(jnp.float32)
    )
    cos_y = jnp.cos(angles_y)
    sin_y = jnp.sin(angles_y)
    upper = jnp.concatenate([cos_y, sin_y], axis=1)
    lower = jnp.concatenate([-sin_y, cos_y], axis=1)
    col_table = jnp.concatenate([upper, lower], axis=0).astype(jnp.bfloat16)
    return (row_table, col_table)


def spectra_of(images, mask_radius, row_table, col_table):
    row_count, pixels, _ = images.shape
    band_size = row_table.shape[1] // 2
    centre = jnp.arange(pixels, dtype=jnp.int32) - pixels // 2
    radius_sq = centre[:, None] * centre[:, None] + centre[None, :] * centre[None, :]
    inside = radius_sq[None, :, :] <= (mask_radius * mask_radius)[:, None, None]
    masked = jnp.where(inside, images, jnp.zeros((), jnp.bfloat16))
    partial_value = jnp.dot(
        masked.reshape(row_count * pixels, pixels), row_table, preferred_element_type=jnp.float32
    )
    partial_value = partial_value.astype(jnp.bfloat16).reshape(row_count, pixels, 2, band_size)
    partial_value = partial_value.transpose(0, 2, 1, 3).reshape(row_count, 2 * pixels, band_size)
    whole = (
        jnp.einsum("ym,pmx->pyx", col_table, partial_value, preferred_element_type=jnp.float32)
        / pixels
    )
    return whole.reshape(row_count, 4 * band_size * band_size).astype(jnp.bfloat16)


def phase_tables(pixels, band_size, side_len):
    freq_y = jnp.arange(2 * band_size, dtype=jnp.int32) - band_size
    freq_x = jnp.arange(band_size, dtype=jnp.int32)
    offsets = jnp.arange(side_len, dtype=jnp.int32) - side_len // 2
    shift_y = jnp.repeat(offsets, side_len)
    horizontal_displacement = jnp.tile(offsets, side_len)
    phase_arg = (
        freq_y[None, :, None] * shift_y[:, None, None]
        + freq_x[None, None, :] * horizontal_displacement[:, None, None]
    ) % pixels
    angles = 2.0 * math.pi / pixels * phase_arg.astype(jnp.float32).reshape(side_len * side_len, -1)
    return (jnp.cos(angles), jnp.sin(angles))


def translated_images(
    reference_block, noise_inverse_power, cosine_lookup_matrix, sine_lookup_matrix
):
    half_len = reference_block.shape[-1] // 2
    real_part = reference_block[:, :half_len].astype(jnp.float32) * noise_inverse_power[None, :]
    imag_part = reference_block[:, half_len:].astype(jnp.float32) * noise_inverse_power[None, :]
    cos_b = cosine_lookup_matrix[:, None, :]
    sin_b = sine_lookup_matrix[:, None, :]
    rot_real = real_part[None] * cos_b - imag_part[None] * sin_b
    turned_sine_term = real_part[None] * sin_b + imag_part[None] * cos_b
    stack = jnp.concatenate([rot_real, turned_sine_term], axis=-1).astype(jnp.bfloat16)
    return stack.reshape(-1, reference_block.shape[-1])


def penalty_lookup(reference_block, noise_inverse_power):
    half_len = reference_block.shape[-1] // 2
    real_part = reference_block[:, :half_len].astype(jnp.float32)
    imag_part = reference_block[:, half_len:].astype(jnp.float32)
    return 0.5 * jnp.sum(
        noise_inverse_power[None, :] * (real_part * real_part + imag_part * imag_part), axis=1
    )


def score_slots(block_spectra, centres, stack, penalty, bias_value, rot_count):
    slot_count = block_spectra.shape[0]
    cross_term = jnp.dot(block_spectra, stack.T, preferred_element_type=jnp.float32)
    cross_term = cross_term.reshape(slot_count, -1, rot_count)
    angle_step = jnp.arange(rot_count, dtype=jnp.float32)[None, :] - centres[:, None]
    prior_term = KAPPA * jnp.cos(2.0 * math.pi / rot_count * angle_step)
    total = cross_term - penalty[None, None, :] + bias_value + prior_term[:, None, :]
    return total.reshape(slot_count, -1)


def shift_back(gathered, cosine_lookup_matrix, sine_lookup_matrix):
    half_len = gathered.shape[-1] // 2
    real_block_part = gathered[..., :half_len]
    imaginary_block_part = gathered[..., half_len:]
    largest_score_seen = lax.Precision.HIGHEST
    real_running_sum = jnp.einsum(
        "iqz,iz->qz", real_block_part, cosine_lookup_matrix, precision=largest_score_seen
    ) + jnp.einsum(
        "iqz,iz->qz", imaginary_block_part, sine_lookup_matrix, precision=largest_score_seen
    )
    imaginary_running_sum = jnp.einsum(
        "iqz,iz->qz", imaginary_block_part, cosine_lookup_matrix, precision=largest_score_seen
    ) - jnp.einsum("iqz,iz->qz", real_block_part, sine_lookup_matrix, precision=largest_score_seen)
    return jnp.concatenate([real_running_sum, imaginary_running_sum], axis=-1)


def routed(
    images, mask_radius, rotation_prior, candidates, references, noise_inverse_power, class_bias
):
    row_count = images.shape[0]
    classes_on_device, rot_count, freq_len = references.shape
    top_count = candidates.shape[1]
    devices = lax.axis_size("cls")
    reference_groups_list = classes_on_device * devices
    maximum_holding = max(2, 2 * row_count * top_count // reference_groups_list)
    hypotheses = SIDE * SIDE * rot_count
    row_table, col_table = dft_tables(images.shape[1], BAND)
    spectra = spectra_of(images, mask_radius, row_table, col_table)
    cosine_lookup_matrix, sine_lookup_matrix = phase_tables(images.shape[1], BAND, SIDE)
    flat_ids = candidates.reshape(-1)
    placement_coordinate = jnp.arange(row_count * top_count, dtype=jnp.int32)
    same = (flat_ids[None, :] == flat_ids[:, None]) & (
        placement_coordinate[None, :] < placement_coordinate[:, None]
    )
    earlier = jnp.sum(same.astype(jnp.int32), axis=1)
    slot_index = flat_ids * maximum_holding + earlier
    filled = (
        jnp.zeros((reference_groups_list * maximum_holding,), jnp.int32)
        .at[slot_index]
        .set(placement_coordinate + 1)
    )
    live_slot = filled > 0
    entry_index = jnp.maximum(filled - 1, 0)
    owner_row = entry_index // top_count
    outgoing = jnp.where(live_slot[:, None], spectra[owner_row], jnp.zeros((), jnp.bfloat16))
    outgoing = outgoing.reshape(devices, classes_on_device, maximum_holding, freq_len)
    centres_out = jnp.where(live_slot, rotation_prior[owner_row], 0).astype(jnp.bfloat16)
    centres_out = centres_out.reshape(devices, classes_on_device, maximum_holding)
    stacks = [
        translated_images(
            references[device_local], noise_inverse_power, cosine_lookup_matrix, sine_lookup_matrix
        )
        for device_local in range(classes_on_device)
    ]
    displacement_costs = [
        penalty_lookup(references[device_local], noise_inverse_power)
        for device_local in range(classes_on_device)
    ]
    arrived, arrived_centres = (
        lax.all_to_all(outgoing, "cls", split_axis=0, concat_axis=0, tiled=True),
        lax.all_to_all(centres_out, "cls", split_axis=0, concat_axis=0, tiled=True),
    )
    sources = arrived.shape[0]
    width = arrived.shape[2]
    blocks = []
    for score_device_local in range(classes_on_device):
        score_block_spectra = arrived[:, score_device_local].reshape(sources * width, freq_len)
        centres = (
            arrived_centres[:, score_device_local].reshape(sources * width).astype(jnp.float32)
        )
        scored = score_slots(
            score_block_spectra,
            centres,
            stacks[score_device_local],
            displacement_costs[score_device_local],
            class_bias[score_device_local],
            rot_count,
        )
        blocks.append(scored.reshape(sources, width, hypotheses))
    scores = jnp.stack(blocks, axis=1)
    returned = lax.all_to_all(scores, "cls", split_axis=0, concat_axis=0, tiled=True)
    self_class_scores = returned.reshape(reference_groups_list * maximum_holding, hypotheses)[
        slot_index
    ]
    per_particle = self_class_scores.reshape(row_count, top_count * hypotheses)
    top_peak = jnp.max(per_particle, axis=1)
    log_norm = top_peak + jnp.log(jnp.sum(jnp.exp(per_particle - top_peak[:, None]), axis=1))
    own_weights = jnp.exp(self_class_scores - jnp.repeat(log_norm, top_count)[:, None]).astype(
        jnp.bfloat16
    )
    weight_buffer = jnp.where(
        live_slot[:, None], own_weights[entry_index], jnp.zeros((), jnp.bfloat16)
    )
    weight_buffer = weight_buffer.reshape(devices, classes_on_device, maximum_holding, hypotheses)
    weights = lax.all_to_all(weight_buffer, "cls", split_axis=0, concat_axis=0, tiled=True)
    output_scale_factor = classes_on_device * rot_count / row_count
    sum_list = []
    occ_list = []
    for device_local in range(classes_on_device):
        block_weights = weights[:, device_local].reshape(-1, hypotheses)
        block_spectra = arrived[:, device_local].reshape(-1, freq_len)
        occupied = jnp.sum(
            block_weights.astype(jnp.float32).reshape(-1, SIDE * SIDE, rot_count), axis=(0, 1)
        )
        occ_list.append(occupied * output_scale_factor)
        gathered = jnp.einsum(
            "sh,sf->hf", block_weights, block_spectra, preferred_element_type=jnp.float32
        )
        gathered = gathered.reshape(SIDE * SIDE, rot_count, freq_len)
        sum_list.append(
            shift_back(gathered, cosine_lookup_matrix, sine_lookup_matrix) * output_scale_factor
        )
    return (jnp.stack(sum_list, axis=0), jnp.stack(occ_list, axis=0), log_norm)


def fused_kernel(
    nd, spec, labs, refs, ninv, cos_t, sin_t, cols, sums, occ, norm_out,
    everyone, labels, pairs, stack, scores, weights, base,
    up_sem, down_sem, x_sem, core_sem, recv_sem, lab_send, lab_recv, pair_send, pair_recv,
):
    me = lax.axis_index("cls")
    part = lax.axis_index("parts")
    nz = nd // 4
    z, x, c = me // 4, me // 2 % 2, me % 2
    shifts = cos_t.shape[0]
    rows = refs.shape[0]
    half = ninv.shape[1]
    group = 4 * spec.shape[0]

    def remote(src, dst, send, recv, peer):
        return pltpu.make_async_remote_copy(
            src_ref=src, dst_ref=dst, send_sem=send, recv_sem=recv,
            device_id=(part, peer), device_id_type=pl.DeviceIdType.MESH,
        )

    barrier = pltpu.get_barrier_semaphore()
    for k in range(1, nd):
        pl.semaphore_signal(
            barrier, inc=1, device_id=(part, (me + k) % nd), device_id_type=pl.DeviceIdType.MESH
        )
    pl.semaphore_wait(barrier, nd - 1)

    def block_copy(o, sem, peer):
        return remote(everyone.at[o], everyone.at[o], sem.at[o], recv_sem.at[o], peer)

    def wait_block(o):
        block_copy(o, x_sem, (me + 1) % nd).wait_recv()

    def sends(zz, act):
        o = zz * 4 + x * 2 + c

        @pl.when((zz <= z) & (z + 1 < nz))
        def _():
            act(block_copy(o, up_sem, me + 4))

        @pl.when((zz >= z) & (z > 0))
        def _():
            act(block_copy(o, down_sem, me - 4))

        act(block_copy(o, x_sem, z * 4 + (1 - x) * 2 + c))
        act(block_copy(o, core_sem, z * 4 + x * 2 + 1 - c))

    def cross_send(zz, act):
        o = zz * 4 + (1 - x) * 2 + c
        act(block_copy(o, core_sem, z * 4 + x * 2 + 1 - c))

    everyone[me] = spec[...]
    sends(z, lambda d: d.start())
    labels[me] = labs[...]
    for k in range(1, nd):
        peer = (me + k) % nd
        remote(labs, labels.at[me], lab_send.at[k], lab_recv.at[me], peer).start()

    tile = 512
    cost = jnp.zeros((rows, 1), jnp.float32)
    for f in range(0, half, tile):
        power = ninv[:, f : f + tile]
        re = refs[:, f : f + tile].astype(jnp.float32)
        im = refs[:, half + f : half + f + tile].astype(jnp.float32)
        cost = cost + jnp.sum(power * (re * re + im * im), axis=1, keepdims=True)
        re = re * power
        im = im * power
        for t in range(shifts):
            ct = cos_t[t : t + 1, f : f + tile]
            st = sin_t[t : t + 1, f : f + tile]
            stack[t * rows : (t + 1) * rows, f : f + tile] = (re * ct - im * st).astype(
                jnp.bfloat16
            )
            stack[t * rows : (t + 1) * rows, half + f : half + f + tile] = (
                re * st + im * ct
            ).astype(jnp.bfloat16)
    base[...] = jnp.broadcast_to(cols[:, 0:1] - 0.5 * cost, base.shape)
    for k in range(1, nd):
        o = (me + k) % nd
        remote(labs, labels.at[o], lab_send.at[k], lab_recv.at[o], o).wait_recv()

    def score_group(zz):
        lanes = pl.ds(pl.multiple_of(zz * group, group), group)
        first = labels[4 * zz] + labels[4 * zz + 1]
        second = labels[4 * zz + 2] + labels[4 * zz + 3]
        lab = jnp.concatenate([first, second], axis=1)
        top_count = lab.shape[0] - 8
        mine = cols[:, 3:4]
        named = lab[0:1, :] == mine
        for k in range(1, top_count):
            named = named | (lab[k : k + 1, :] == mine)
        extra = (
            base[:, 0:1]
            + cols[:, 1:2] * lab[top_count : top_count + 1, :]
            + cols[:, 2:3] * lab[top_count + 1 : top_count + 2, :]
        )
        block = everyone[pl.ds(4 * zz, 4)].reshape(group, spec.shape[1])
        step = 3 * rows

        def chunk(i, top):
            at = pl.multiple_of(i * step, step)
            value = lax.dot_general(
                stack[pl.ds(at, step), :], block, (((1,), (1,)), ((), ())),
                preferred_element_type=jnp.float32,
            )
            for j in range(3):
                one = jnp.where(named, value[j * rows : (j + 1) * rows] + extra, LOWEST)
                scores[pl.ds(pl.multiple_of(at + j * rows, rows), rows), lanes] = one
                top = jnp.maximum(top, one)
            return top

        top = lax.fori_loop(
            0, shifts // 3, chunk, jnp.full((rows, group), LOWEST, jnp.float32)
        )
        top = jnp.max(top, axis=0, keepdims=True)
        mass = jnp.zeros((rows, group), jnp.float32)
        for t in range(shifts):
            mass = mass + jnp.exp(scores[t * rows : (t + 1) * rows, lanes] - top)
        pairs[me, 0:1, lanes] = top
        pairs[me, 1:2, lanes] = jnp.sum(mass, axis=0, keepdims=True)

    def at_distance(s, fn):
        @pl.when(z - s >= 0)
        def _():
            fn(z - s)

        @pl.when((s > 0) & (z + s < nz))
        def _():
            fn(z + s)

    def from_column(zz):
        wait_block(zz * 4 + x * 2 + c)
        sends(zz, lambda d: d.start())

    def from_side(zz):
        wait_block(zz * 4 + (1 - x) * 2 + c)
        cross_send(zz, lambda d: d.start())

    def finish_group(zz):
        wait_block(zz * 4 + x * 2 + 1 - c)
        wait_block(zz * 4 + (1 - x) * 2 + 1 - c)
        score_group(zz)

    def stage(i, carry):
        @pl.when(i < nz)
        def _():
            at_distance(i, from_column)

        at_distance(i - 1, from_side)
        at_distance(i - 1, finish_group)
        return carry

    lax.fori_loop(1, nz + 1, stage, 0)

    for k in range(1, nd):
        peer = (me + k) % nd
        remote(pairs.at[me], pairs.at[me], pair_send.at[k], pair_recv.at[me], peer).start()
    for k in range(1, nd):
        o = (me + k) % nd
        remote(pairs.at[o], pairs.at[o], pair_send.at[k], pair_recv.at[o], o).wait_recv()
    peak = pairs[0, 0:1, :]
    for d in range(1, nd):
        peak = jnp.maximum(peak, pairs[d, 0:1, :])
    total = jnp.zeros_like(peak)
    for d in range(nd):
        total = total + pairs[d, 1:2, :] * jnp.exp(pairs[d, 0:1, :] - peak)
    norm = peak + jnp.log(total)
    norm_out[...] = norm
    scale = cols[0:1, 4:5]

    def weigh(t, held):
        at = pl.ds(pl.multiple_of(t * rows, rows), rows)
        w = jnp.exp(scores[at, :] - norm_out[...]).astype(jnp.bfloat16)
        weights[at, :] = w
        return held + jnp.sum(w.astype(jnp.float32), axis=1, keepdims=True)

    held = lax.fori_loop(0, shifts, weigh, jnp.zeros((rows, 1), jnp.float32))
    occ[...] = jnp.broadcast_to(held * scale, occ.shape)

    wide = 256

    def back(i, carry):
        at = pl.multiple_of(i * wide, wide)
        re_at, im_at = pl.ds(at, wide), pl.ds(pl.multiple_of(half + at, wide), wide)
        re = everyone[:, :, re_at].reshape(-1, wide)
        im = everyone[:, :, im_at].reshape(-1, wide)
        g_re = jnp.dot(weights[...], re, preferred_element_type=jnp.float32)
        g_im = jnp.dot(weights[...], im, preferred_element_type=jnp.float32)
        out_re = jnp.zeros((rows, wide), jnp.float32)
        out_im = jnp.zeros((rows, wide), jnp.float32)
        for t in range(shifts):
            ct = cos_t[t : t + 1, re_at]
            st = sin_t[t : t + 1, re_at]
            a = g_re[t * rows : (t + 1) * rows]
            b = g_im[t * rows : (t + 1) * rows]
            out_re = out_re + a * ct + b * st
            out_im = out_im + b * ct - a * st
        sums[:, re_at] = out_re * scale
        sums[:, im_at] = out_im * scale
        return carry

    lax.fori_loop(0, half // wide, back, 0)

    def settle(zz, carry):
        sends(zz, lambda d: d.wait_send())
        cross_send(zz, lambda d: d.wait_send())
        return carry

    lax.fori_loop(0, nz, settle, 0)
    for k in range(1, nd):
        peer = (me + k) % nd
        remote(labs, labels.at[me], lab_send.at[k], lab_recv.at[me], peer).wait_send()
        remote(pairs.at[me], pairs.at[me], pair_send.at[k], pair_recv.at[me], peer).wait_send()


def phase_constants(pixels, band_size, side_len):
    fy = np.arange(2 * band_size) - band_size
    fx = np.arange(band_size)
    off = np.arange(side_len) - side_len // 2
    a, b = np.repeat(off, side_len), np.tile(off, side_len)
    arg = (fy[None, :, None] * a[:, None, None] + fx[None, None, :] * b[:, None, None]) % pixels
    ang = 2.0 * math.pi / pixels * arg.reshape(side_len * side_len, -1)
    return np.cos(ang).astype(np.float32), np.sin(ang).astype(np.float32)


def dense(
    images, mask_radius, rotation_prior, candidates, references, noise_inverse_power, class_bias
):
    row_count, top_count = candidates.shape
    classes_on_device, rot_count, freq_len = references.shape
    devices = lax.axis_size("cls")
    me = lax.axis_index("cls")
    particles = devices * row_count
    rows = classes_on_device * rot_count
    shifts = SIDE * SIDE
    row_table, col_table = dft_tables(images.shape[1], BAND)
    spectra = spectra_of(images, mask_radius, row_table, col_table)
    cos_t, sin_t = phase_constants(images.shape[1], BAND, SIDE)
    turn = 2.0 * math.pi / rot_count
    angle = turn * rotation_prior.astype(jnp.float32)
    labs = jnp.concatenate(
        [
            candidates.T.astype(jnp.float32),
            KAPPA * jnp.cos(angle)[None],
            KAPPA * jnp.sin(angle)[None],
            jnp.zeros((6, row_count), jnp.float32),
        ],
        axis=0,
    )
    blank = jnp.zeros_like(labs)
    labs = jnp.where(
        me % 2 == 0,
        jnp.concatenate([labs, blank], axis=1),
        jnp.concatenate([blank, labs], axis=1),
    )
    r = np.arange(rows) % rot_count
    own = (me * classes_on_device + jnp.arange(rows) // rot_count).astype(jnp.float32)
    scale = classes_on_device * rot_count / row_count
    cols = jnp.stack(
        [
            jnp.repeat(class_bias, rot_count),
            jnp.asarray(np.cos(turn * r), jnp.float32),
            jnp.asarray(np.sin(turn * r), jnp.float32),
            own,
            jnp.full((rows,), scale, jnp.float32),
        ],
        axis=1,
    )
    cols = jnp.pad(cols, ((0, 0), (0, 123)))
    vmem = pl.BlockSpec(memory_space=pltpu.VMEM)
    dma = pltpu.SemaphoreType.DMA((devices,))
    sums, occ, norm = pl.pallas_call(
        functools.partial(fused_kernel, devices),
        out_shape=(
            jax.ShapeDtypeStruct((rows, freq_len), jnp.float32),
            jax.ShapeDtypeStruct((rows, 128), jnp.float32),
            jax.ShapeDtypeStruct((1, particles), jnp.float32),
        ),
        in_specs=[vmem] * 7,
        out_specs=(vmem, vmem, vmem),
        scratch_shapes=[
            pltpu.VMEM((devices, row_count, freq_len), jnp.bfloat16),
            pltpu.VMEM((devices,) + labs.shape, jnp.float32),
            pltpu.VMEM((devices, 2, particles), jnp.float32),
            pltpu.VMEM((shifts * rows, freq_len), jnp.bfloat16),
            pltpu.VMEM((shifts * rows, particles), jnp.float32),
            pltpu.VMEM((shifts * rows, particles), jnp.bfloat16),
            pltpu.VMEM((rows, 128), jnp.float32),
        ]
        + [dma] * 9,
        compiler_params=pltpu.CompilerParams(
            collective_id=0, has_side_effects=True, vmem_limit_bytes=52 * 1024 * 1024
        ),
    )(
        spectra,
        labs,
        references.reshape(rows, freq_len),
        noise_inverse_power[None],
        jnp.asarray(cos_t),
        jnp.asarray(sin_t),
        cols,
    )
    own_norm = lax.dynamic_slice(norm[0], (me * row_count,), (row_count,))
    return (
        sums.reshape(classes_on_device, rot_count, freq_len),
        occ[:, 0].reshape(classes_on_device, rot_count),
        own_norm,
    )


def local(*arrays):
    row_count, top_count = arrays[3].shape
    devices = lax.axis_size("cls")
    classes = arrays[4].shape[0] * devices
    slots = max(2, 2 * row_count * top_count // classes)
    fits = row_count == 64 and devices % 4 == 0 and row_count <= 2 * slots
    return dense(*arrays) if fits else routed(*arrays)


def solution(mesh):
    in_specs = (
        P(("parts", "cls"), None, None),
        P(("parts", "cls")),
        P(("parts", "cls")),
        P(("parts", "cls"), None),
        P(("parts", "cls"), None, None),
        P(),
        P(("parts", "cls")),
    )
    out_specs = (P(("parts", "cls"), None, None), P(("parts", "cls"), None), P(("parts", "cls")))
    return jax.shard_map(local, mesh=mesh, in_specs=in_specs, out_specs=out_specs, check_vma=False)
```

```python
import functools
import math

import jax
import jax.numpy as jnp
import numpy as np
from jax import lax
from jax.experimental import pallas as pl
from jax.experimental.pallas import tpu as pltpu
from jax.sharding import PartitionSpec as P

BAND = 32
SIDE = 3


KAPPA = 2.0
LOWEST = -1e30
LATE = 20


def dft_tables(pixels, band_size):
    pixel_idx = jnp.arange(pixels, dtype=jnp.int32)
    freq_x = jnp.arange(band_size, dtype=jnp.int32)
    angles_x = (
        2.0 * math.pi / pixels * (pixel_idx[:, None] * freq_x[None, :] % pixels).astype(jnp.float32)
    )
    row_table = jnp.concatenate([jnp.cos(angles_x), -jnp.sin(angles_x)], axis=1).astype(
        jnp.bfloat16
    )
    freq_y = jnp.arange(2 * band_size, dtype=jnp.int32) - band_size
    angles_y = (
        2.0 * math.pi / pixels * (freq_y[:, None] * pixel_idx[None, :] % pixels).astype(jnp.float32)
    )
    cos_y = jnp.cos(angles_y)
    sin_y = jnp.sin(angles_y)
    upper = jnp.concatenate([cos_y, sin_y], axis=1)
    lower = jnp.concatenate([-sin_y, cos_y], axis=1)
    col_table = jnp.concatenate([upper, lower], axis=0).astype(jnp.bfloat16)
    return (row_table, col_table)


def spectra_of(images, mask_radius, row_table, col_table):
    row_count, pixels, _ = images.shape
    band_size = row_table.shape[1] // 2
    centre = jnp.arange(pixels, dtype=jnp.int32) - pixels // 2
    radius_sq = centre[:, None] * centre[:, None] + centre[None, :] * centre[None, :]
    inside = radius_sq[None, :, :] <= (mask_radius * mask_radius)[:, None, None]
    masked = jnp.where(inside, images, jnp.zeros((), jnp.bfloat16))
    partial_value = jnp.dot(
        masked.reshape(row_count * pixels, pixels), row_table, preferred_element_type=jnp.float32
    )
    partial_value = partial_value.astype(jnp.bfloat16).reshape(row_count, pixels, 2, band_size)
    partial_value = partial_value.transpose(0, 2, 1, 3).reshape(row_count, 2 * pixels, band_size)
    whole = (
        jnp.einsum("ym,pmx->pyx", col_table, partial_value, preferred_element_type=jnp.float32)
        / pixels
    )
    return whole.reshape(row_count, 4 * band_size * band_size).astype(jnp.bfloat16)


def phase_tables(pixels, band_size, side_len):
    freq_y = jnp.arange(2 * band_size, dtype=jnp.int32) - band_size
    freq_x = jnp.arange(band_size, dtype=jnp.int32)
    offsets = jnp.arange(side_len, dtype=jnp.int32) - side_len // 2
    shift_y = jnp.repeat(offsets, side_len)
    horizontal_displacement = jnp.tile(offsets, side_len)
    phase_arg = (
        freq_y[None, :, None] * shift_y[:, None, None]
        + freq_x[None, None, :] * horizontal_displacement[:, None, None]
    ) % pixels
    angles = 2.0 * math.pi / pixels * phase_arg.astype(jnp.float32).reshape(side_len * side_len, -1)
    return (jnp.cos(angles), jnp.sin(angles))


def translated_images(
    reference_block, noise_inverse_power, cosine_lookup_matrix, sine_lookup_matrix
):
    half_len = reference_block.shape[-1] // 2
    real_part = reference_block[:, :half_len].astype(jnp.float32) * noise_inverse_power[None, :]
    imag_part = reference_block[:, half_len:].astype(jnp.float32) * noise_inverse_power[None, :]
    cos_b = cosine_lookup_matrix[:, None, :]
    sin_b = sine_lookup_matrix[:, None, :]
    rot_real = real_part[None] * cos_b - imag_part[None] * sin_b
    turned_sine_term = real_part[None] * sin_b + imag_part[None] * cos_b
    stack = jnp.concatenate([rot_real, turned_sine_term], axis=-1).astype(jnp.bfloat16)
    return stack.reshape(-1, reference_block.shape[-1])


def penalty_lookup(reference_block, noise_inverse_power):
    half_len = reference_block.shape[-1] // 2
    real_part = reference_block[:, :half_len].astype(jnp.float32)
    imag_part = reference_block[:, half_len:].astype(jnp.float32)
    return 0.5 * jnp.sum(
        noise_inverse_power[None, :] * (real_part * real_part + imag_part * imag_part), axis=1
    )


def score_slots(block_spectra, centres, stack, penalty, bias_value, rot_count):
    slot_count = block_spectra.shape[0]
    cross_term = jnp.dot(block_spectra, stack.T, preferred_element_type=jnp.float32)
    cross_term = cross_term.reshape(slot_count, -1, rot_count)
    angle_step = jnp.arange(rot_count, dtype=jnp.float32)[None, :] - centres[:, None]
    prior_term = KAPPA * jnp.cos(2.0 * math.pi / rot_count * angle_step)
    total = cross_term - penalty[None, None, :] + bias_value + prior_term[:, None, :]
    return total.reshape(slot_count, -1)


def shift_back(gathered, cosine_lookup_matrix, sine_lookup_matrix):
    half_len = gathered.shape[-1] // 2
    real_block_part = gathered[..., :half_len]
    imaginary_block_part = gathered[..., half_len:]
    largest_score_seen = lax.Precision.HIGHEST
    real_running_sum = jnp.einsum(
        "iqz,iz->qz", real_block_part, cosine_lookup_matrix, precision=largest_score_seen
    ) + jnp.einsum(
        "iqz,iz->qz", imaginary_block_part, sine_lookup_matrix, precision=largest_score_seen
    )
    imaginary_running_sum = jnp.einsum(
        "iqz,iz->qz", imaginary_block_part, cosine_lookup_matrix, precision=largest_score_seen
    ) - jnp.einsum("iqz,iz->qz", real_block_part, sine_lookup_matrix, precision=largest_score_seen)
    return jnp.concatenate([real_running_sum, imaginary_running_sum], axis=-1)


def routed(
    images, mask_radius, rotation_prior, candidates, references, noise_inverse_power, class_bias
):
    row_count = images.shape[0]
    classes_on_device, rot_count, freq_len = references.shape
    top_count = candidates.shape[1]
    devices = lax.axis_size("cls")
    reference_groups_list = classes_on_device * devices
    maximum_holding = max(2, 2 * row_count * top_count // reference_groups_list)
    hypotheses = SIDE * SIDE * rot_count
    row_table, col_table = dft_tables(images.shape[1], BAND)
    spectra = spectra_of(images, mask_radius, row_table, col_table)
    cosine_lookup_matrix, sine_lookup_matrix = phase_tables(images.shape[1], BAND, SIDE)
    flat_ids = candidates.reshape(-1)
    placement_coordinate = jnp.arange(row_count * top_count, dtype=jnp.int32)
    same = (flat_ids[None, :] == flat_ids[:, None]) & (
        placement_coordinate[None, :] < placement_coordinate[:, None]
    )
    earlier = jnp.sum(same.astype(jnp.int32), axis=1)
    slot_index = flat_ids * maximum_holding + earlier
    filled = (
        jnp.zeros((reference_groups_list * maximum_holding,), jnp.int32)
        .at[slot_index]
        .set(placement_coordinate + 1)
    )
    live_slot = filled > 0
    entry_index = jnp.maximum(filled - 1, 0)
    owner_row = entry_index // top_count
    outgoing = jnp.where(live_slot[:, None], spectra[owner_row], jnp.zeros((), jnp.bfloat16))
    outgoing = outgoing.reshape(devices, classes_on_device, maximum_holding, freq_len)
    centres_out = jnp.where(live_slot, rotation_prior[owner_row], 0).astype(jnp.bfloat16)
    centres_out = centres_out.reshape(devices, classes_on_device, maximum_holding)
    stacks = [
        translated_images(
            references[device_local], noise_inverse_power, cosine_lookup_matrix, sine_lookup_matrix
        )
        for device_local in range(classes_on_device)
    ]
    displacement_costs = [
        penalty_lookup(references[device_local], noise_inverse_power)
        for device_local in range(classes_on_device)
    ]
    arrived, arrived_centres = (
        lax.all_to_all(outgoing, "cls", split_axis=0, concat_axis=0, tiled=True),
        lax.all_to_all(centres_out, "cls", split_axis=0, concat_axis=0, tiled=True),
    )
    sources = arrived.shape[0]
    width = arrived.shape[2]
    blocks = []
    for score_device_local in range(classes_on_device):
        score_block_spectra = arrived[:, score_device_local].reshape(sources * width, freq_len)
        centres = (
            arrived_centres[:, score_device_local].reshape(sources * width).astype(jnp.float32)
        )
        scored = score_slots(
            score_block_spectra,
            centres,
            stacks[score_device_local],
            displacement_costs[score_device_local],
            class_bias[score_device_local],
            rot_count,
        )
        blocks.append(scored.reshape(sources, width, hypotheses))
    scores = jnp.stack(blocks, axis=1)
    returned = lax.all_to_all(scores, "cls", split_axis=0, concat_axis=0, tiled=True)
    self_class_scores = returned.reshape(reference_groups_list * maximum_holding, hypotheses)[
        slot_index
    ]
    per_particle = self_class_scores.reshape(row_count, top_count * hypotheses)
    top_peak = jnp.max(per_particle, axis=1)
    log_norm = top_peak + jnp.log(jnp.sum(jnp.exp(per_particle - top_peak[:, None]), axis=1))
    own_weights = jnp.exp(self_class_scores - jnp.repeat(log_norm, top_count)[:, None]).astype(
        jnp.bfloat16
    )
    weight_buffer = jnp.where(
        live_slot[:, None], own_weights[entry_index], jnp.zeros((), jnp.bfloat16)
    )
    weight_buffer = weight_buffer.reshape(devices, classes_on_device, maximum_holding, hypotheses)
    weights = lax.all_to_all(weight_buffer, "cls", split_axis=0, concat_axis=0, tiled=True)
    output_scale_factor = classes_on_device * rot_count / row_count
    sum_list = []
    occ_list = []
    for device_local in range(classes_on_device):
        block_weights = weights[:, device_local].reshape(-1, hypotheses)
        block_spectra = arrived[:, device_local].reshape(-1, freq_len)
        occupied = jnp.sum(
            block_weights.astype(jnp.float32).reshape(-1, SIDE * SIDE, rot_count), axis=(0, 1)
        )
        occ_list.append(occupied * output_scale_factor)
        gathered = jnp.einsum(
            "sh,sf->hf", block_weights, block_spectra, preferred_element_type=jnp.float32
        )
        gathered = gathered.reshape(SIDE * SIDE, rot_count, freq_len)
        sum_list.append(
            shift_back(gathered, cosine_lookup_matrix, sine_lookup_matrix) * output_scale_factor
        )
    return (jnp.stack(sum_list, axis=0), jnp.stack(occ_list, axis=0), log_norm)


def fused_kernel(
    nd, spec, names, refs, ninv, cos_t, sin_t, cols, bias, sums, occ, norm_out,
    everyone, labels, pairs, stack, scores, weights, base, labs,
    up_sem, down_sem, x_sem, core_sem, recv_sem, late_sem, lab_send, lab_recv, pair_send, pair_recv,
):
    me = lax.axis_index("cls")
    part = lax.axis_index("parts")
    nz = nd // 4
    z, x, c = me // 4, me // 2 % 2, me % 2
    shifts = cos_t.shape[0]
    rows = refs.shape[0]
    half = ninv.shape[1]
    group = 4 * spec.shape[0]
    keep = spec.shape[1] - spec.shape[1] * LATE // 128 // 128 * 128

    def remote(src, dst, send, recv, peer):
        return pltpu.make_async_remote_copy(
            src_ref=src, dst_ref=dst, send_sem=send, recv_sem=recv,
            device_id=(part, peer), device_id_type=pl.DeviceIdType.MESH,
        )

    barrier = pltpu.get_barrier_semaphore()
    for k in range(1, nd):
        pl.semaphore_signal(
            barrier, inc=1, device_id=(part, (me + k) % nd), device_id_type=pl.DeviceIdType.MESH
        )
    pl.semaphore_wait(barrier, nd - 1)

    def block_copy(o, sem, peer):
        return remote(everyone.at[o], everyone.at[o], sem.at[o], recv_sem.at[o], peer)

    def wait_block(o):
        block_copy(o, x_sem, (me + 1) % nd).wait_recv()

    def late_copy(o, sem, peer):
        piece = everyone.at[o, :, keep:]
        return remote(piece, piece, sem.at[o], late_sem.at[o], peer)

    def late_sends(zz, act):
        o = zz * 4 + (1 - x) * 2 + c

        @pl.when((zz <= z) & (z + 1 < nz))
        def _():
            act(late_copy(o, up_sem, me + 4))

        @pl.when((zz >= z) & (z > 0))
        def _():
            act(late_copy(o, down_sem, me - 4))

    def side_copy(o, peer):
        piece = everyone.at[o, :, :keep]
        return remote(piece, piece, x_sem.at[o], recv_sem.at[o], peer)

    def sends(zz, act):
        o = zz * 4 + x * 2 + c

        @pl.when((zz <= z) & (z + 1 < nz))
        def _():
            act(block_copy(o, up_sem, me + 4))

        @pl.when((zz >= z) & (z > 0))
        def _():
            act(block_copy(o, down_sem, me - 4))

        @pl.when(zz == z)
        def _():
            act(block_copy(o, x_sem, z * 4 + (1 - x) * 2 + c))

        @pl.when(zz != z)
        def _():
            act(side_copy(o, z * 4 + (1 - x) * 2 + c))

        act(block_copy(o, core_sem, z * 4 + x * 2 + 1 - c))

    def cross_send(zz, act):
        o = zz * 4 + (1 - x) * 2 + c
        act(block_copy(o, core_sem, z * 4 + x * 2 + 1 - c))

    everyone[me] = spec[...]
    sends(z, lambda d: d.start())
    count = names.shape[0]
    place = lax.broadcasted_iota(jnp.int32, (count, 2 * count), 1) - count * c
    place = place == lax.broadcasted_iota(jnp.int32, (count, 2 * count), 0)
    labs[...] = lax.dot_general(
        names[...], place.astype(jnp.float32).astype(jnp.bfloat16), (((0,), (0,)), ((), ())),
        preferred_element_type=jnp.float32,
    )
    labels[me] = labs[...]
    for k in range(1, nd):
        peer = (me + k) % nd
        remote(labs, labels.at[me], lab_send.at[k], lab_recv.at[me], peer).start()

    tile = 512
    cost = jnp.zeros((rows, 1), jnp.float32)
    for f in range(0, half, tile):
        power = ninv[:, f : f + tile]
        re = refs[:, f : f + tile].astype(jnp.float32)
        im = refs[:, half + f : half + f + tile].astype(jnp.float32)
        cost = cost + jnp.sum(power * (re * re + im * im), axis=1, keepdims=True)
        re = re * power
        im = im * power
        for t in range(shifts):
            ct = cos_t[t : t + 1, f : f + tile]
            st = sin_t[t : t + 1, f : f + tile]
            stack[t * rows : (t + 1) * rows, f : f + tile] = (re * ct - im * st).astype(
                jnp.bfloat16
            )
            stack[t * rows : (t + 1) * rows, half + f : half + f + tile] = (
                re * st + im * ct
            ).astype(jnp.bfloat16)
    own = cols[:, 2:3]
    offset = -0.5 * cost
    for k in range(bias.shape[0]):
        offset = offset + jnp.where(own == k, bias[k], 0.0)
    base[...] = jnp.broadcast_to(offset, base.shape)
    for k in range(1, nd):
        o = (me + k) % nd
        remote(labs, labels.at[o], lab_send.at[k], lab_recv.at[o], o).wait_recv()

    def score_group(zz):
        lanes = pl.ds(pl.multiple_of(zz * group, group), group)
        first = labels[4 * zz] + labels[4 * zz + 1]
        second = labels[4 * zz + 2] + labels[4 * zz + 3]
        lab = jnp.concatenate([first, second], axis=1)
        top_count = lab.shape[0] - 8
        mine = cols[:, 2:3] + (me * bias.shape[0]).astype(jnp.float32)
        named = lab[0:1, :] == mine
        for k in range(1, top_count):
            named = named | (lab[k : k + 1, :] == mine)
        angle = 2.0 * math.pi / (rows // bias.shape[0]) * lab[top_count : top_count + 1, :]
        extra = (
            base[:, 0:1]
            + cols[:, 0:1] * (KAPPA * jnp.cos(angle))
            + cols[:, 1:2] * (KAPPA * jnp.sin(angle))
        )
        block = everyone[pl.ds(4 * zz, 4)].reshape(group, spec.shape[1])
        step = 3 * rows

        def chunk(i, top):
            at = pl.multiple_of(i * step, step)
            value = lax.dot_general(
                stack[pl.ds(at, step), :], block, (((1,), (1,)), ((), ())),
                preferred_element_type=jnp.float32,
            )
            for j in range(3):
                one = jnp.where(named, value[j * rows : (j + 1) * rows] + extra, LOWEST)
                scores[pl.ds(pl.multiple_of(at + j * rows, rows), rows), lanes] = one
                top = jnp.maximum(top, one)
            return top

        top = lax.fori_loop(
            0, shifts // 3, chunk, jnp.full((rows, group), LOWEST, jnp.float32)
        )
        top = jnp.max(top, axis=0, keepdims=True)
        mass = jnp.zeros((rows, group), jnp.float32)
        for t in range(shifts):
            mass = mass + jnp.exp(scores[t * rows : (t + 1) * rows, lanes] - top)
        pairs[me, 0:1, lanes] = top
        pairs[me, 1:2, lanes] = jnp.sum(mass, axis=0, keepdims=True)

    def at_distance(s, fn):
        @pl.when(z - s >= 0)
        def _():
            fn(z - s)

        @pl.when((s > 0) & (z + s < nz))
        def _():
            fn(z + s)

    def from_column(zz):
        wait_block(zz * 4 + x * 2 + c)
        sends(zz, lambda d: d.start())

    def from_late(zz):
        o = zz * 4 + (1 - x) * 2 + c

        @pl.when(zz == z)
        def _():
            wait_block(o)

        @pl.when(zz != z)
        def _():
            late_copy(o, up_sem, (me + 1) % nd).wait_recv()

        late_sends(zz, lambda d: d.start())

    def from_side(zz):
        o = zz * 4 + (1 - x) * 2 + c

        @pl.when(zz != z)
        def _():
            side_copy(o, (me + 1) % nd).wait_recv()

        cross_send(zz, lambda d: d.start())

    def finish_group(zz):
        wait_block(zz * 4 + x * 2 + 1 - c)
        wait_block(zz * 4 + (1 - x) * 2 + 1 - c)
        score_group(zz)

    def stage(i, carry):
        @pl.when(i < nz)
        def _():
            at_distance(i, from_column)

        at_distance(i - 1, from_late)
        at_distance(i - 1, from_side)
        at_distance(i - 1, finish_group)
        return carry

    lax.fori_loop(1, nz + 1, stage, 0)

    for k in range(1, nd):
        peer = (me + k) % nd
        remote(pairs.at[me], pairs.at[me], pair_send.at[k], pair_recv.at[me], peer).start()
    for k in range(1, nd):
        o = (me + k) % nd
        remote(pairs.at[o], pairs.at[o], pair_send.at[k], pair_recv.at[o], o).wait_recv()
    peak = pairs[0, 0:1, :]
    for d in range(1, nd):
        peak = jnp.maximum(peak, pairs[d, 0:1, :])
    total = jnp.zeros_like(peak)
    for d in range(nd):
        total = total + pairs[d, 1:2, :] * jnp.exp(pairs[d, 0:1, :] - peak)
    norm = peak + jnp.log(total)
    norm_out[...] = norm
    scale = bias.shape[0] * (rows // bias.shape[0]) / count

    def weigh(t, held):
        at = pl.ds(pl.multiple_of(t * rows, rows), rows)
        w = jnp.exp(scores[at, :] - norm_out[...]).astype(jnp.bfloat16)
        weights[at, :] = w
        return held + jnp.sum(w.astype(jnp.float32), axis=1, keepdims=True)

    held = lax.fori_loop(0, shifts, weigh, jnp.zeros((rows, 1), jnp.float32))
    occ[...] = jnp.broadcast_to(held * scale, occ.shape)

    wide = 256

    def back(i, carry):
        at = pl.multiple_of(i * wide, wide)
        re_at, im_at = pl.ds(at, wide), pl.ds(pl.multiple_of(half + at, wide), wide)
        re = everyone[:, :, re_at].reshape(-1, wide)
        im = everyone[:, :, im_at].reshape(-1, wide)
        g_re = jnp.dot(weights[...], re, preferred_element_type=jnp.float32)
        g_im = jnp.dot(weights[...], im, preferred_element_type=jnp.float32)
        out_re = jnp.zeros((rows, wide), jnp.float32)
        out_im = jnp.zeros((rows, wide), jnp.float32)
        for t in range(shifts):
            ct = cos_t[t : t + 1, re_at]
            st = sin_t[t : t + 1, re_at]
            a = g_re[t * rows : (t + 1) * rows]
            b = g_im[t * rows : (t + 1) * rows]
            out_re = out_re + a * ct + b * st
            out_im = out_im + b * ct - a * st
        sums[:, re_at] = out_re
        sums[:, im_at] = out_im
        return carry

    lax.fori_loop(0, half // wide, back, 0)

    def settle(zz, carry):
        sends(zz, lambda d: d.wait_send())
        late_sends(zz, lambda d: d.wait_send())
        cross_send(zz, lambda d: d.wait_send())
        return carry

    lax.fori_loop(0, nz, settle, 0)
    for k in range(1, nd):
        peer = (me + k) % nd
        remote(labs, labels.at[me], lab_send.at[k], lab_recv.at[me], peer).wait_send()
        remote(pairs.at[me], pairs.at[me], pair_send.at[k], pair_recv.at[me], peer).wait_send()


def phase_constants(pixels, band_size, side_len):
    fy = np.arange(2 * band_size) - band_size
    fx = np.arange(band_size)
    off = np.arange(side_len) - side_len // 2
    a, b = np.repeat(off, side_len), np.tile(off, side_len)
    arg = (fy[None, :, None] * a[:, None, None] + fx[None, None, :] * b[:, None, None]) % pixels
    ang = 2.0 * math.pi / pixels * arg.reshape(side_len * side_len, -1)
    return np.cos(ang).astype(np.float32), np.sin(ang).astype(np.float32)


def dense(
    images, mask_radius, rotation_prior, candidates, references, noise_inverse_power, class_bias
):
    row_count, top_count = candidates.shape
    classes_on_device, rot_count, freq_len = references.shape
    devices = lax.axis_size("cls")
    me = lax.axis_index("cls")
    particles = devices * row_count
    rows = classes_on_device * rot_count
    shifts = SIDE * SIDE
    row_table, col_table = dft_tables(images.shape[1], BAND)
    spectra = spectra_of(images, mask_radius, row_table, col_table)
    cos_t, sin_t = phase_constants(images.shape[1], BAND, SIDE)
    names = jnp.concatenate([candidates, rotation_prior[:, None]], axis=1)
    names = jnp.pad(names, ((0, 0), (0, 7))).astype(jnp.bfloat16)
    r = np.arange(rows)
    turn = 2.0 * math.pi / rot_count * (r % rot_count)
    cols = np.zeros((rows, 128), np.float32)
    cols[:, 0], cols[:, 1], cols[:, 2] = np.cos(turn), np.sin(turn), r // rot_count
    scale = classes_on_device * rot_count / row_count
    vmem = pl.BlockSpec(memory_space=pltpu.VMEM)
    dma = pltpu.SemaphoreType.DMA((devices,))
    sums, occ, norm = pl.pallas_call(
        functools.partial(fused_kernel, devices),
        out_shape=(
            jax.ShapeDtypeStruct((rows, freq_len), jnp.float32),
            jax.ShapeDtypeStruct((rows, 128), jnp.float32),
            jax.ShapeDtypeStruct((1, particles), jnp.float32),
        ),
        in_specs=[vmem] * 7 + [pl.BlockSpec(memory_space=pltpu.SMEM)],
        out_specs=(vmem, vmem, vmem),
        scratch_shapes=[
            pltpu.VMEM((devices, row_count, freq_len), jnp.bfloat16),
            pltpu.VMEM((devices, top_count + 8, 2 * row_count), jnp.float32),
            pltpu.VMEM((devices, 2, particles), jnp.float32),
            pltpu.VMEM((shifts * rows, freq_len), jnp.bfloat16),
            pltpu.VMEM((shifts * rows, particles), jnp.float32),
            pltpu.VMEM((shifts * rows, particles), jnp.bfloat16),
            pltpu.VMEM((rows, 128), jnp.float32),
            pltpu.VMEM((top_count + 8, 2 * row_count), jnp.float32),
        ]
        + [dma] * 10,
        compiler_params=pltpu.CompilerParams(
            collective_id=0, has_side_effects=True, vmem_limit_bytes=52 * 1024 * 1024
        ),
    )(
        spectra,
        names,
        references.reshape(rows, freq_len),
        noise_inverse_power[None],
        jnp.asarray(cos_t),
        jnp.asarray(sin_t),
        jnp.asarray(cols),
        class_bias,
    )
    own_norm = lax.dynamic_slice(norm[0], (me * row_count,), (row_count,))
    return (
        sums.reshape(classes_on_device, rot_count, freq_len) * scale,
        occ[:, 0].reshape(classes_on_device, rot_count),
        own_norm,
    )


def local(*arrays):
    row_count, top_count = arrays[3].shape
    devices = lax.axis_size("cls")
    classes = arrays[4].shape[0] * devices
    slots = max(2, 2 * row_count * top_count // classes)
    fits = row_count == 64 and devices % 4 == 0 and row_count <= 2 * slots
    return dense(*arrays) if fits else routed(*arrays)


def solution(mesh):
    in_specs = (
        P(("parts", "cls"), None, None),
        P(("parts", "cls")),
        P(("parts", "cls")),
        P(("parts", "cls"), None),
        P(("parts", "cls"), None, None),
        P(),
        P(("parts", "cls")),
    )
    out_specs = (P(("parts", "cls"), None, None), P(("parts", "cls"), None), P(("parts", "cls")))
    return jax.shard_map(local, mesh=mesh, in_specs=in_specs, out_specs=out_specs, check_vma=False)
```

```python
import functools
import math

import jax
import jax.numpy as jnp
import numpy as np
from jax import lax
from jax.experimental import pallas as pl
from jax.experimental.pallas import tpu as pltpu
from jax.sharding import PartitionSpec as P

BAND = 32
SIDE = 3


KAPPA = 2.0
LOWEST = -1e30
LATE = 8


def dft_tables(pixels, band_size):
    pixel_idx = jnp.arange(pixels, dtype=jnp.int32)
    freq_x = jnp.arange(band_size, dtype=jnp.int32)
    angles_x = (
        2.0 * math.pi / pixels * (pixel_idx[:, None] * freq_x[None, :] % pixels).astype(jnp.float32)
    )
    row_table = jnp.concatenate([jnp.cos(angles_x), -jnp.sin(angles_x)], axis=1).astype(
        jnp.bfloat16
    )
    freq_y = jnp.arange(2 * band_size, dtype=jnp.int32) - band_size
    angles_y = (
        2.0 * math.pi / pixels * (freq_y[:, None] * pixel_idx[None, :] % pixels).astype(jnp.float32)
    )
    cos_y = jnp.cos(angles_y)
    sin_y = jnp.sin(angles_y)
    upper = jnp.concatenate([cos_y, sin_y], axis=1)
    lower = jnp.concatenate([-sin_y, cos_y], axis=1)
    col_table = jnp.concatenate([upper, lower], axis=0).astype(jnp.bfloat16)
    return (row_table, col_table)


def spectra_of(images, mask_radius, row_table, col_table):
    row_count, pixels, _ = images.shape
    band_size = row_table.shape[1] // 2
    centre = jnp.arange(pixels, dtype=jnp.int32) - pixels // 2
    radius_sq = centre[:, None] * centre[:, None] + centre[None, :] * centre[None, :]
    inside = radius_sq[None, :, :] <= (mask_radius * mask_radius)[:, None, None]
    masked = jnp.where(inside, images, jnp.zeros((), jnp.bfloat16))
    partial_value = jnp.dot(
        masked.reshape(row_count * pixels, pixels), row_table, preferred_element_type=jnp.float32
    )
    partial_value = partial_value.astype(jnp.bfloat16).reshape(row_count, pixels, 2, band_size)
    partial_value = partial_value.transpose(0, 2, 1, 3).reshape(row_count, 2 * pixels, band_size)
    whole = (
        jnp.einsum("ym,pmx->pyx", col_table, partial_value, preferred_element_type=jnp.float32)
        / pixels
    )
    return whole.reshape(row_count, 4 * band_size * band_size).astype(jnp.bfloat16)


def phase_tables(pixels, band_size, side_len):
    freq_y = jnp.arange(2 * band_size, dtype=jnp.int32) - band_size
    freq_x = jnp.arange(band_size, dtype=jnp.int32)
    offsets = jnp.arange(side_len, dtype=jnp.int32) - side_len // 2
    shift_y = jnp.repeat(offsets, side_len)
    horizontal_displacement = jnp.tile(offsets, side_len)
    phase_arg = (
        freq_y[None, :, None] * shift_y[:, None, None]
        + freq_x[None, None, :] * horizontal_displacement[:, None, None]
    ) % pixels
    angles = 2.0 * math.pi / pixels * phase_arg.astype(jnp.float32).reshape(side_len * side_len, -1)
    return (jnp.cos(angles), jnp.sin(angles))


def translated_images(
    reference_block, noise_inverse_power, cosine_lookup_matrix, sine_lookup_matrix
):
    half_len = reference_block.shape[-1] // 2
    real_part = reference_block[:, :half_len].astype(jnp.float32) * noise_inverse_power[None, :]
    imag_part = reference_block[:, half_len:].astype(jnp.float32) * noise_inverse_power[None, :]
    cos_b = cosine_lookup_matrix[:, None, :]
    sin_b = sine_lookup_matrix[:, None, :]
    rot_real = real_part[None] * cos_b - imag_part[None] * sin_b
    turned_sine_term = real_part[None] * sin_b + imag_part[None] * cos_b
    stack = jnp.concatenate([rot_real, turned_sine_term], axis=-1).astype(jnp.bfloat16)
    return stack.reshape(-1, reference_block.shape[-1])


def penalty_lookup(reference_block, noise_inverse_power):
    half_len = reference_block.shape[-1] // 2
    real_part = reference_block[:, :half_len].astype(jnp.float32)
    imag_part = reference_block[:, half_len:].astype(jnp.float32)
    return 0.5 * jnp.sum(
        noise_inverse_power[None, :] * (real_part * real_part + imag_part * imag_part), axis=1
    )


def score_slots(block_spectra, centres, stack, penalty, bias_value, rot_count):
    slot_count = block_spectra.shape[0]
    cross_term = jnp.dot(block_spectra, stack.T, preferred_element_type=jnp.float32)
    cross_term = cross_term.reshape(slot_count, -1, rot_count)
    angle_step = jnp.arange(rot_count, dtype=jnp.float32)[None, :] - centres[:, None]
    prior_term = KAPPA * jnp.cos(2.0 * math.pi / rot_count * angle_step)
    total = cross_term - penalty[None, None, :] + bias_value + prior_term[:, None, :]
    return total.reshape(slot_count, -1)


def shift_back(gathered, cosine_lookup_matrix, sine_lookup_matrix):
    half_len = gathered.shape[-1] // 2
    real_block_part = gathered[..., :half_len]
    imaginary_block_part = gathered[..., half_len:]
    largest_score_seen = lax.Precision.HIGHEST
    real_running_sum = jnp.einsum(
        "iqz,iz->qz", real_block_part, cosine_lookup_matrix, precision=largest_score_seen
    ) + jnp.einsum(
        "iqz,iz->qz", imaginary_block_part, sine_lookup_matrix, precision=largest_score_seen
    )
    imaginary_running_sum = jnp.einsum(
        "iqz,iz->qz", imaginary_block_part, cosine_lookup_matrix, precision=largest_score_seen
    ) - jnp.einsum("iqz,iz->qz", real_block_part, sine_lookup_matrix, precision=largest_score_seen)
    return jnp.concatenate([real_running_sum, imaginary_running_sum], axis=-1)


def routed(
    images, mask_radius, rotation_prior, candidates, references, noise_inverse_power, class_bias
):
    row_count = images.shape[0]
    classes_on_device, rot_count, freq_len = references.shape
    top_count = candidates.shape[1]
    devices = lax.axis_size("cls")
    reference_groups_list = classes_on_device * devices
    maximum_holding = max(2, 2 * row_count * top_count // reference_groups_list)
    hypotheses = SIDE * SIDE * rot_count
    row_table, col_table = dft_tables(images.shape[1], BAND)
    spectra = spectra_of(images, mask_radius, row_table, col_table)
    cosine_lookup_matrix, sine_lookup_matrix = phase_tables(images.shape[1], BAND, SIDE)
    flat_ids = candidates.reshape(-1)
    placement_coordinate = jnp.arange(row_count * top_count, dtype=jnp.int32)
    same = (flat_ids[None, :] == flat_ids[:, None]) & (
        placement_coordinate[None, :] < placement_coordinate[:, None]
    )
    earlier = jnp.sum(same.astype(jnp.int32), axis=1)
    slot_index = flat_ids * maximum_holding + earlier
    filled = (
        jnp.zeros((reference_groups_list * maximum_holding,), jnp.int32)
        .at[slot_index]
        .set(placement_coordinate + 1)
    )
    live_slot = filled > 0
    entry_index = jnp.maximum(filled - 1, 0)
    owner_row = entry_index // top_count
    outgoing = jnp.where(live_slot[:, None], spectra[owner_row], jnp.zeros((), jnp.bfloat16))
    outgoing = outgoing.reshape(devices, classes_on_device, maximum_holding, freq_len)
    centres_out = jnp.where(live_slot, rotation_prior[owner_row], 0).astype(jnp.bfloat16)
    centres_out = centres_out.reshape(devices, classes_on_device, maximum_holding)
    stacks = [
        translated_images(
            references[device_local], noise_inverse_power, cosine_lookup_matrix, sine_lookup_matrix
        )
        for device_local in range(classes_on_device)
    ]
    displacement_costs = [
        penalty_lookup(references[device_local], noise_inverse_power)
        for device_local in range(classes_on_device)
    ]
    arrived, arrived_centres = (
        lax.all_to_all(outgoing, "cls", split_axis=0, concat_axis=0, tiled=True),
        lax.all_to_all(centres_out, "cls", split_axis=0, concat_axis=0, tiled=True),
    )
    sources = arrived.shape[0]
    width = arrived.shape[2]
    blocks = []
    for score_device_local in range(classes_on_device):
        score_block_spectra = arrived[:, score_device_local].reshape(sources * width, freq_len)
        centres = (
            arrived_centres[:, score_device_local].reshape(sources * width).astype(jnp.float32)
        )
        scored = score_slots(
            score_block_spectra,
            centres,
            stacks[score_device_local],
            displacement_costs[score_device_local],
            class_bias[score_device_local],
            rot_count,
        )
        blocks.append(scored.reshape(sources, width, hypotheses))
    scores = jnp.stack(blocks, axis=1)
    returned = lax.all_to_all(scores, "cls", split_axis=0, concat_axis=0, tiled=True)
    self_class_scores = returned.reshape(reference_groups_list * maximum_holding, hypotheses)[
        slot_index
    ]
    per_particle = self_class_scores.reshape(row_count, top_count * hypotheses)
    top_peak = jnp.max(per_particle, axis=1)
    log_norm = top_peak + jnp.log(jnp.sum(jnp.exp(per_particle - top_peak[:, None]), axis=1))
    own_weights = jnp.exp(self_class_scores - jnp.repeat(log_norm, top_count)[:, None]).astype(
        jnp.bfloat16
    )
    weight_buffer = jnp.where(
        live_slot[:, None], own_weights[entry_index], jnp.zeros((), jnp.bfloat16)
    )
    weight_buffer = weight_buffer.reshape(devices, classes_on_device, maximum_holding, hypotheses)
    weights = lax.all_to_all(weight_buffer, "cls", split_axis=0, concat_axis=0, tiled=True)
    output_scale_factor = classes_on_device * rot_count / row_count
    sum_list = []
    occ_list = []
    for device_local in range(classes_on_device):
        block_weights = weights[:, device_local].reshape(-1, hypotheses)
        block_spectra = arrived[:, device_local].reshape(-1, freq_len)
        occupied = jnp.sum(
            block_weights.astype(jnp.float32).reshape(-1, SIDE * SIDE, rot_count), axis=(0, 1)
        )
        occ_list.append(occupied * output_scale_factor)
        gathered = jnp.einsum(
            "sh,sf->hf", block_weights, block_spectra, preferred_element_type=jnp.float32
        )
        gathered = gathered.reshape(SIDE * SIDE, rot_count, freq_len)
        sum_list.append(
            shift_back(gathered, cosine_lookup_matrix, sine_lookup_matrix) * output_scale_factor
        )
    return (jnp.stack(sum_list, axis=0), jnp.stack(occ_list, axis=0), log_norm)


def fused_kernel(
    nd, spec, names, refs, ninv, cos_t, sin_t, cols, bias, sums, occ, norm_out,
    everyone, labels, pairs, stack, scores, weights, base, labs,
    up_sem, down_sem, x_sem, core_sem, recv_sem, late_sem, lab_send, lab_recv, pair_send, pair_recv,
):
    me = lax.axis_index("cls")
    part = lax.axis_index("parts")
    nz = nd // 4
    z, x, c = me // 4, me // 2 % 2, me % 2
    shifts = cos_t.shape[0]
    rows = refs.shape[0]
    half = ninv.shape[1]
    group = 4 * spec.shape[0]
    keep = spec.shape[1] - spec.shape[1] * LATE // 128 // 128 * 128

    def remote(src, dst, send, recv, peer):
        return pltpu.make_async_remote_copy(
            src_ref=src, dst_ref=dst, send_sem=send, recv_sem=recv,
            device_id=(part, peer), device_id_type=pl.DeviceIdType.MESH,
        )

    barrier = pltpu.get_barrier_semaphore()
    for k in range(1, nd):
        pl.semaphore_signal(
            barrier, inc=1, device_id=(part, (me + k) % nd), device_id_type=pl.DeviceIdType.MESH
        )
    pl.semaphore_wait(barrier, nd - 1)

    def block_copy(o, sem, peer):
        return remote(everyone.at[o], everyone.at[o], sem.at[o], recv_sem.at[o], peer)

    def wait_block(o):
        block_copy(o, x_sem, (me + 1) % nd).wait_recv()

    def late_copy(o, sem, peer):
        piece = everyone.at[o, :, keep:]
        return remote(piece, piece, sem.at[o], late_sem.at[o], peer)

    def late_sends(zz, act):
        o = zz * 4 + (1 - x) * 2 + c

        @pl.when((zz <= z) & (z + 1 < nz))
        def _():
            act(late_copy(o, up_sem, me + 4))

        @pl.when((zz >= z) & (z > 0))
        def _():
            act(late_copy(o, down_sem, me - 4))

    def side_copy(o, peer):
        piece = everyone.at[o, :, :keep]
        return remote(piece, piece, x_sem.at[o], recv_sem.at[o], peer)

    def sends(zz, act):
        o = zz * 4 + x * 2 + c

        @pl.when((zz <= z) & (z + 1 < nz))
        def _():
            act(block_copy(o, up_sem, me + 4))

        @pl.when((zz >= z) & (z > 0))
        def _():
            act(block_copy(o, down_sem, me - 4))

        @pl.when(zz == z)
        def _():
            act(block_copy(o, x_sem, z * 4 + (1 - x) * 2 + c))

        @pl.when(zz != z)
        def _():
            act(side_copy(o, z * 4 + (1 - x) * 2 + c))

        act(block_copy(o, core_sem, z * 4 + x * 2 + 1 - c))

    def cross_send(zz, act):
        o = zz * 4 + (1 - x) * 2 + c
        act(block_copy(o, core_sem, z * 4 + x * 2 + 1 - c))

    everyone[me] = spec[...]
    sends(z, lambda d: d.start())
    count = names.shape[0]
    place = lax.broadcasted_iota(jnp.int32, (count, 2 * count), 1) - count * c
    place = place == lax.broadcasted_iota(jnp.int32, (count, 2 * count), 0)
    labs[...] = lax.dot_general(
        names[...], place.astype(jnp.float32).astype(jnp.bfloat16), (((0,), (0,)), ((), ())),
        preferred_element_type=jnp.float32,
    )
    labels[me] = labs[...]
    for k in range(1, nd):
        peer = (me + k) % nd
        remote(labs, labels.at[me], lab_send.at[k], lab_recv.at[me], peer).start()

    tile = 512
    cost = jnp.zeros((rows, 1), jnp.float32)
    for f in range(0, half, tile):
        power = ninv[:, f : f + tile]
        re = refs[:, f : f + tile].astype(jnp.float32)
        im = refs[:, half + f : half + f + tile].astype(jnp.float32)
        cost = cost + jnp.sum(power * (re * re + im * im), axis=1, keepdims=True)
        re = re * power
        im = im * power
        for t in range(shifts):
            ct = cos_t[t : t + 1, f : f + tile]
            st = sin_t[t : t + 1, f : f + tile]
            stack[t * rows : (t + 1) * rows, f : f + tile] = (re * ct - im * st).astype(
                jnp.bfloat16
            )
            stack[t * rows : (t + 1) * rows, half + f : half + f + tile] = (
                re * st + im * ct
            ).astype(jnp.bfloat16)
    own = cols[:, 2:3]
    offset = -0.5 * cost
    for k in range(bias.shape[0]):
        offset = offset + jnp.where(own == k, bias[k], 0.0)
    base[...] = jnp.broadcast_to(offset, base.shape)
    for k in range(1, nd):
        o = (me + k) % nd
        remote(labs, labels.at[o], lab_send.at[k], lab_recv.at[o], o).wait_recv()

    def score_group(zz):
        lanes = pl.ds(pl.multiple_of(zz * group, group), group)
        first = labels[4 * zz] + labels[4 * zz + 1]
        second = labels[4 * zz + 2] + labels[4 * zz + 3]
        lab = jnp.concatenate([first, second], axis=1)
        top_count = lab.shape[0] - 8
        mine = cols[:, 2:3] + (me * bias.shape[0]).astype(jnp.float32)
        named = lab[0:1, :] == mine
        for k in range(1, top_count):
            named = named | (lab[k : k + 1, :] == mine)
        angle = 2.0 * math.pi / (rows // bias.shape[0]) * lab[top_count : top_count + 1, :]
        extra = (
            base[:, 0:1]
            + cols[:, 0:1] * (KAPPA * jnp.cos(angle))
            + cols[:, 1:2] * (KAPPA * jnp.sin(angle))
        )
        block = everyone[pl.ds(4 * zz, 4)].reshape(group, spec.shape[1])
        step = 3 * rows

        def chunk(i, top):
            at = pl.multiple_of(i * step, step)
            value = lax.dot_general(
                stack[pl.ds(at, step), :], block, (((1,), (1,)), ((), ())),
                preferred_element_type=jnp.float32,
            )
            for j in range(3):
                one = jnp.where(named, value[j * rows : (j + 1) * rows] + extra, LOWEST)
                scores[pl.ds(pl.multiple_of(at + j * rows, rows), rows), lanes] = one
                top = jnp.maximum(top, one)
            return top

        top = lax.fori_loop(
            0, shifts // 3, chunk, jnp.full((rows, group), LOWEST, jnp.float32)
        )
        top = jnp.max(top, axis=0, keepdims=True)
        mass = jnp.zeros((rows, group), jnp.float32)
        for t in range(shifts):
            mass = mass + jnp.exp(scores[t * rows : (t + 1) * rows, lanes] - top)
        pairs[me, 0:1, lanes] = top
        pairs[me, 1:2, lanes] = jnp.sum(mass, axis=0, keepdims=True)

    def at_distance(s, fn):
        @pl.when(z - s >= 0)
        def _():
            fn(z - s)

        @pl.when((s > 0) & (z + s < nz))
        def _():
            fn(z + s)

    def from_column(zz):
        wait_block(zz * 4 + x * 2 + c)
        sends(zz, lambda d: d.start())

    def from_late(zz):
        o = zz * 4 + (1 - x) * 2 + c

        @pl.when(zz == z)
        def _():
            wait_block(o)

        @pl.when(zz != z)
        def _():
            late_copy(o, up_sem, (me + 1) % nd).wait_recv()

        late_sends(zz, lambda d: d.start())

    def from_side(zz):
        o = zz * 4 + (1 - x) * 2 + c

        @pl.when(zz != z)
        def _():
            side_copy(o, (me + 1) % nd).wait_recv()

        cross_send(zz, lambda d: d.start())

    def finish_group(zz):
        wait_block(zz * 4 + x * 2 + 1 - c)
        wait_block(zz * 4 + (1 - x) * 2 + 1 - c)
        score_group(zz)

    def stage(i, carry):
        @pl.when(i < nz)
        def _():
            at_distance(i, from_column)

        at_distance(i - 1, from_late)
        at_distance(i - 1, from_side)
        at_distance(i - 1, finish_group)
        return carry

    lax.fori_loop(1, nz + 1, stage, 0)

    for k in range(1, nd):
        peer = (me + k) % nd
        remote(pairs.at[me], pairs.at[me], pair_send.at[k], pair_recv.at[me], peer).start()
    for k in range(1, nd):
        o = (me + k) % nd
        remote(pairs.at[o], pairs.at[o], pair_send.at[k], pair_recv.at[o], o).wait_recv()
    peak = pairs[0, 0:1, :]
    for d in range(1, nd):
        peak = jnp.maximum(peak, pairs[d, 0:1, :])
    total = jnp.zeros_like(peak)
    for d in range(nd):
        total = total + pairs[d, 1:2, :] * jnp.exp(pairs[d, 0:1, :] - peak)
    norm = peak + jnp.log(total)
    norm_out[...] = norm
    scale = bias.shape[0] * (rows // bias.shape[0]) / count

    def weigh(t, held):
        at = pl.ds(pl.multiple_of(t * rows, rows), rows)
        w = jnp.exp(scores[at, :] - norm_out[...]).astype(jnp.bfloat16)
        weights[at, :] = w
        return held + jnp.sum(w.astype(jnp.float32), axis=1, keepdims=True)

    held = lax.fori_loop(0, shifts, weigh, jnp.zeros((rows, 1), jnp.float32))
    occ[...] = jnp.broadcast_to(held * scale, occ.shape)

    wide = 256

    def back(i, carry):
        at = pl.multiple_of(i * wide, wide)
        re_at, im_at = pl.ds(at, wide), pl.ds(pl.multiple_of(half + at, wide), wide)
        re = everyone[:, :, re_at].reshape(-1, wide)
        im = everyone[:, :, im_at].reshape(-1, wide)
        g_re = jnp.dot(weights[...], re, preferred_element_type=jnp.float32)
        g_im = jnp.dot(weights[...], im, preferred_element_type=jnp.float32)
        out_re = jnp.zeros((rows, wide), jnp.float32)
        out_im = jnp.zeros((rows, wide), jnp.float32)
        for t in range(shifts):
            ct = cos_t[t : t + 1, re_at]
            st = sin_t[t : t + 1, re_at]
            a = g_re[t * rows : (t + 1) * rows]
            b = g_im[t * rows : (t + 1) * rows]
            out_re = out_re + a * ct + b * st
            out_im = out_im + b * ct - a * st
        sums[:, re_at] = out_re
        sums[:, im_at] = out_im
        return carry

    lax.fori_loop(0, half // wide, back, 0, unroll=2)

    def settle(zz, carry):
        sends(zz, lambda d: d.wait_send())
        late_sends(zz, lambda d: d.wait_send())
        cross_send(zz, lambda d: d.wait_send())
        return carry

    lax.fori_loop(0, nz, settle, 0)
    for k in range(1, nd):
        peer = (me + k) % nd
        remote(labs, labels.at[me], lab_send.at[k], lab_recv.at[me], peer).wait_send()
        remote(pairs.at[me], pairs.at[me], pair_send.at[k], pair_recv.at[me], peer).wait_send()


def phase_constants(pixels, band_size, side_len):
    fy = np.arange(2 * band_size) - band_size
    fx = np.arange(band_size)
    off = np.arange(side_len) - side_len // 2
    a, b = np.repeat(off, side_len), np.tile(off, side_len)
    arg = (fy[None, :, None] * a[:, None, None] + fx[None, None, :] * b[:, None, None]) % pixels
    ang = 2.0 * math.pi / pixels * arg.reshape(side_len * side_len, -1)
    return np.cos(ang).astype(np.float32), np.sin(ang).astype(np.float32)


def dense(
    images, mask_radius, rotation_prior, candidates, references, noise_inverse_power, class_bias
):
    row_count, top_count = candidates.shape
    classes_on_device, rot_count, freq_len = references.shape
    devices = lax.axis_size("cls")
    me = lax.axis_index("cls")
    particles = devices * row_count
    rows = classes_on_device * rot_count
    shifts = SIDE * SIDE
    row_table, col_table = dft_tables(images.shape[1], BAND)
    spectra = spectra_of(images, mask_radius, row_table, col_table)
    cos_t, sin_t = phase_constants(images.shape[1], BAND, SIDE)
    names = jnp.concatenate([candidates, rotation_prior[:, None]], axis=1)
    names = jnp.pad(names, ((0, 0), (0, 7))).astype(jnp.bfloat16)
    r = np.arange(rows)
    turn = 2.0 * math.pi / rot_count * (r % rot_count)
    cols = np.zeros((rows, 128), np.float32)
    cols[:, 0], cols[:, 1], cols[:, 2] = np.cos(turn), np.sin(turn), r // rot_count
    scale = classes_on_device * rot_count / row_count
    vmem = pl.BlockSpec(memory_space=pltpu.VMEM)
    dma = pltpu.SemaphoreType.DMA((devices,))
    sums, occ, norm = pl.pallas_call(
        functools.partial(fused_kernel, devices),
        out_shape=(
            jax.ShapeDtypeStruct((rows, freq_len), jnp.float32),
            jax.ShapeDtypeStruct((rows, 128), jnp.float32),
            jax.ShapeDtypeStruct((1, particles), jnp.float32),
        ),
        in_specs=[vmem] * 7 + [pl.BlockSpec(memory_space=pltpu.SMEM)],
        out_specs=(vmem, vmem, vmem),
        scratch_shapes=[
            pltpu.VMEM((devices, row_count, freq_len), jnp.bfloat16),
            pltpu.VMEM((devices, top_count + 8, 2 * row_count), jnp.float32),
            pltpu.VMEM((devices, 2, particles), jnp.float32),
            pltpu.VMEM((shifts * rows, freq_len), jnp.bfloat16),
            pltpu.VMEM((shifts * rows, particles), jnp.float32),
            pltpu.VMEM((shifts * rows, particles), jnp.bfloat16),
            pltpu.VMEM((rows, 128), jnp.float32),
            pltpu.VMEM((top_count + 8, 2 * row_count), jnp.float32),
        ]
        + [dma] * 10,
        compiler_params=pltpu.CompilerParams(
            collective_id=0, has_side_effects=True, vmem_limit_bytes=52 * 1024 * 1024
        ),
    )(
        spectra,
        names,
        references.reshape(rows, freq_len),
        noise_inverse_power[None],
        jnp.asarray(cos_t),
        jnp.asarray(sin_t),
        jnp.asarray(cols),
        class_bias,
    )
    own_norm = lax.dynamic_slice(norm[0], (me * row_count,), (row_count,))
    return (
        sums.reshape(classes_on_device, rot_count, freq_len) * scale,
        occ[:, 0].reshape(classes_on_device, rot_count),
        own_norm,
    )


def local(*arrays):
    row_count, top_count = arrays[3].shape
    devices = lax.axis_size("cls")
    classes = arrays[4].shape[0] * devices
    slots = max(2, 2 * row_count * top_count // classes)
    fits = row_count == 64 and devices % 4 == 0 and row_count <= 2 * slots
    return dense(*arrays) if fits else routed(*arrays)


def solution(mesh):
    in_specs = (
        P(("parts", "cls"), None, None),
        P(("parts", "cls")),
        P(("parts", "cls")),
        P(("parts", "cls"), None),
        P(("parts", "cls"), None, None),
        P(),
        P(("parts", "cls")),
    )
    out_specs = (P(("parts", "cls"), None, None), P(("parts", "cls"), None), P(("parts", "cls")))
    return jax.shard_map(local, mesh=mesh, in_specs=in_specs, out_specs=out_specs, check_vma=False)
```
